128 devices in a mesh: img: 8 (over x, core), txt: 16 (over y, z).
Axes of the slice: x: 4, y: 4, z: 4, core: 2. Of those that a mesh axis runs over, the one named last changes fastest.
Arguments:
- image_feat: float32 [16384, 1280], P(('img', 'txt')), may hold values from -1 to 1
- text_feat: float32 [16384, 1280], P(('txt', 'img')), may hold values from -1 to 1
- logit_temp: float32 [], replicated, may hold values from 4.4 to 4.6
Outputs:
- mean_loss: float32 [], replicated
- grad_image: float32 [16384, 1280], P(('img', 'txt'))
- grad_text: float32 [16384, 1280], P(('txt', 'img'))
- temp_grad: float32 [], replicated
The draws below stay inside these ranges and needn't reach their ends.
All inputs are finite; a program needn't handle non-finite values.
Results may differ from the reference program's by a relative error of at most 0.013.
Values may be sent and summed in bfloat16 or wider, within the bound.
A program may use at most 128 MiB of HBM per device.

```python
import math
import jax
import jax.numpy as jnp
from jax import lax

E = 1280
PAIRS = 16384


def shared_rows(key):
    return jax.random.truncated_normal(key, -4.0, 4.0, (PAIRS, E), jnp.float32)


def draw_image_feat(key, part):
    shared = shared_rows(key)
    key = jax.random.fold_in(key, 11)
    scales = jnp.exp(jax.random.uniform(key, (PAIRS, 1), jnp.float32, -1.0, 1.0))
    return jnp.clip(shared * scales * E ** (-0.5), -1.0, 1.0)


def draw_text_feat(key, part):
    shared = shared_rows(key)
    key = jax.random.fold_in(key, 23)
    jitter = jax.random.truncated_normal(key, -4.0, 4.0, (PAIRS, E), jnp.float32)
    scales = jnp.exp(jax.random.uniform(jax.random.fold_in(key, 5), (PAIRS, 1), jnp.float32, -1.0, 1.0))
    blended = 0.2 * shared + 0.98 * jitter
    return jnp.clip(blended * scales * E ** (-0.5), -1.0, 1.0)


def draw_logit_temp(key, part):
    key = jax.random.fold_in(key, 37)
    return jax.random.uniform(key, (), jnp.float32, 4.4, 4.6)


def setup_inputs(seed: int = 0) -> dict:
    keys = jax.random.split(jax.random.key(seed), 4)
    return {
        "image_feat": draw_image_feat(jax.random.fold_in(keys[3], 71), 0),
        "text_feat": draw_text_feat(jax.random.fold_in(keys[3], 71), 0),
        "logit_temp": draw_logit_temp(jax.random.fold_in(keys[3], 71), 0),
    }


def contract_rows(left, right):
    return lax.dot_general(left, right, (((1,), (1,)), ((), ())), precision=lax.Precision.HIGHEST, preferred_element_type=jnp.float32)

def contract_cols(left, right):
    return lax.dot_general(left, right, (((0,), (0,)), ((), ())), precision=lax.Precision.HIGHEST, preferred_element_type=jnp.float32)

def unit_rows(features):
    inverse = lax.rsqrt(lax.optimization_barrier(jnp.sum(features * features, axis=1, keepdims=True)) + 1e-06)
    return (features * inverse, inverse)

def log_sum_exp(scores):
    peak_value = lax.optimization_barrier(jnp.max(scores, axis=1))
    return peak_value + jnp.log(lax.optimization_barrier(jnp.sum(jnp.exp(scores - peak_value[:, None]), axis=1)))

def reference(image_feat, text_feat, logit_temp):
    image_unit, image_inverse = unit_rows(image_feat)
    text_unit, text_inverse = unit_rows(text_feat)
    image_wide = image_unit.astype(jnp.bfloat16).astype(jnp.float32)
    text_wide = text_unit.astype(jnp.bfloat16).astype(jnp.float32)
    logit_scale = jnp.exp(logit_temp)
    block_rows = math.gcd(PAIRS, 512)
    image_blocks = image_wide.reshape(-1, block_rows, E)
    text_blocks = text_wide.reshape(-1, block_rows, E)

    def row_stats(row_block):
        return log_sum_exp(logit_scale * contract_rows(row_block, text_wide))

    def col_stats(col_block):
        return log_sum_exp(logit_scale * contract_rows(col_block, image_wide))
    row_lse = lax.map(row_stats, image_blocks).reshape(-1)
    col_lse = lax.map(col_stats, text_blocks).reshape(-1)
    diag_scores = logit_scale * lax.optimization_barrier(jnp.sum(image_wide * text_wide, axis=1))
    mean_loss = (jnp.sum(row_lse) + jnp.sum(col_lse) - 2.0 * jnp.sum(diag_scores)) / (2.0 * PAIRS)
    all_ids = jnp.arange(PAIRS, dtype=jnp.int32)
    block_ids = all_ids.reshape(-1, block_rows)

    def image_side(item):
        row_block, lse_block, row_ids = item
        scores = logit_scale * contract_rows(row_block, text_wide)
        mask = row_ids[:, None] == all_ids[None, :]
        weights = 0.5 * (jnp.exp(scores - lse_block[:, None]) + jnp.exp(scores - col_lse[None, :])) - jnp.where(mask, 1.0, 0.0)
        weights = weights.astype(jnp.bfloat16).astype(jnp.float32)
        return logit_scale * jnp.dot(weights, text_wide, precision=lax.Precision.HIGHEST, preferred_element_type=jnp.float32)

    def text_side(item):
        col_block, lse_block, col_ids = item
        scores = logit_scale * contract_rows(image_wide, col_block)
        mask = all_ids[:, None] == col_ids[None, :]
        weights = 0.5 * (jnp.exp(scores - row_lse[:, None]) + jnp.exp(scores - lse_block[None, :])) - jnp.where(mask, 1.0, 0.0)
        weights = weights.astype(jnp.bfloat16).astype(jnp.float32)
        return logit_scale * contract_cols(weights, image_wide)
    image_grad = lax.map(image_side, (image_blocks, row_lse.reshape(-1, block_rows), block_ids)).reshape(PAIRS, E)
    text_grad = lax.map(text_side, (text_blocks, col_lse.reshape(-1, block_rows), block_ids)).reshape(PAIRS, E)
    grad_image = image_inverse * (image_grad - image_unit * lax.optimization_barrier(jnp.sum(image_unit * image_grad, axis=1, keepdims=True)))
    grad_text = text_inverse * (text_grad - text_unit * lax.optimization_barrier(jnp.sum(text_unit * text_grad, axis=1, keepdims=True)))
    temp_grad = jnp.sum(image_wide * image_grad) / PAIRS
    return (mean_loss, grad_image, grad_text, temp_grad)
```

```python
import jax
import jax.numpy as jnp
from jax import lax
from jax.experimental import pallas as pl
from jax.experimental.pallas import tpu as pltpu
from jax.sharding import PartitionSpec as P

PLACE = {(0, 0): 0, (0, 1): 1, (1, 0): 2, (3, 0): 3, (1, 1): 4, (3, 1): 5, (2, 0): 6, (2, 1): 7}
BLOCK = 128
HALF = 64
WIDTH = 1280
GROUP = 256
LOG2E = 1.4426950408889634
LN2 = 0.6931471805599453
HIGH_SHIFT = 33.0
LOW_SHIFT = 86.0
LOW_CAP = 20.0
HIGH_LEAST = 2.0**-62
F32 = jnp.float32
BF16 = jnp.bfloat16


def mod4(v):
    return lax.rem(v + 4, 4)


class Copies:
    def __init__(self, send_sems, recv_sems):
        self.send_sems, self.recv_sems = send_sems, recv_sems
        self.table = {}

    def start(self, name, src, dst, device):
        index = len(self.table)
        copy = pltpu.make_async_remote_copy(
            src_ref=src,
            dst_ref=dst,
            send_sem=self.send_sems.at[index],
            recv_sem=self.recv_sems.at[index],
            device_id=device,
            device_id_type=pl.DeviceIdType.MESH,
        )
        copy.start()
        self.table[name] = copy

    def arrived(self, name):
        self.table[name].wait_recv()

    def finish(self):
        for copy in self.table.values():
            copy.wait_send()


def kernel(
    scale_ref,
    image_ref,
    text_ref,
    grad_image_ref,
    grad_text_ref,
    scalars_ref,
    img,
    txt,
    dots,
    wts,
    row1,
    row2,
    col1,
    col2,
    row_shift,
    col_shift,
    img_stats,
    txt_stats,
    sums_a,
    sums_b,
    img_acc,
    txt_acc,
    img_out,
    txt_out,
    core_out,
    img_in,
    txt_in,
    core_in,
    send_sems,
    recv_sems,
):
    img_index = lax.axis_index("img")
    txt_index = lax.axis_index("txt")
    x, core = img_index // 2, lax.rem(img_index, 2)
    y, z = txt_index // 4, lax.rem(txt_index, 4)
    odd = lax.rem(z, 2)
    z_img = z + 1 - 2 * odd
    z_txt = mod4(z - 1 + 2 * odd)

    def img_peer(r, q):
        return (img_index, mod4(y + r) * 4 + (z_img if q else z))

    def txt_peer(r, q, c=0):
        return (
            mod4(x + r) * 2 + (1 - core if c else core),
            y * 4 + (z_txt if q else z),
        )

    img_offsets = [(r, q) for r in range(4) for q in range(2) if (r, q) != (0, 0)]
    txt_offsets = [
        (r, q, c) for r in range(4) for q in range(2) for c in range(2) if (r, q, c) != (0, 0, 0)
    ]
    barrier = pltpu.get_barrier_semaphore()
    for offset in img_offsets:
        pl.semaphore_signal(barrier, inc=1, device_id=img_peer(*offset), device_id_type=pl.DeviceIdType.MESH)
    for offset in txt_offsets:
        pl.semaphore_signal(barrier, inc=1, device_id=txt_peer(*offset), device_id_type=pl.DeviceIdType.MESH)

    scale = scale_ref[0, 0]
    slope = scale * LOG2E

    def inverse_of(rows):
        return lax.rsqrt(jnp.sum(rows * rows, axis=1, keepdims=True) + 1e-06)

    def normalize(step, carry):
        part = pl.ds(pl.multiple_of(step * 16, 16), 16)
        for source, target in ((image_ref, img), (text_ref, txt)):
            rows = source[part, :]
            target[part, :] = (rows * inverse_of(rows)).astype(BF16)
        return carry

    lax.fori_loop(0, BLOCK // 16, normalize, 0)
    pl.semaphore_wait(barrier, len(img_offsets) + len(txt_offsets))

    copies = Copies(send_sems, recv_sems)

    def half(place, part):
        return pl.ds(place * BLOCK + part * HALF, HALF)

    sides = (("i", img, img_peer), ("t", txt, txt_peer))

    def push(side, name, place, part, to_place, r, q):
        label, rows, peer = side
        copies.start(
            label + name + "ab"[part], rows.at[half(place, part)], rows.at[half(to_place, part)], peer(r, q)
        )

    def to_core(place, part):
        copies.start(
            "c%d%d" % (place, part),
            txt.at[half(place, part)],
            txt.at[half(8 + place, part)],
            txt_peer(0, 0, 1),
        )

    for first in range(2):
        for side in sides:
            push(side, "up", 0, first, PLACE[3, 0], 1, 0)
            push(side, "down", 0, 1 - first, PLACE[1, 0], 3, 0)
            push(side, "z", 0, first, PLACE[0, 1], 0, 1)
        to_core(0, first)

    row1[...] = jnp.zeros_like(row1)
    row2[...] = jnp.zeros_like(row2)
    col1[...] = jnp.zeros_like(col1)
    col2[...] = jnp.zeros_like(col2)

    def forward(row, row_count, column, column_count):
        cols = pl.ds(column, column_count)
        dots[pl.ds(row, row_count), cols] = lax.dot_general(
            img[pl.ds(row, row_count), :],
            txt[cols, :],
            (((1,), (1,)), ((), ())),
            preferred_element_type=F32,
        )

        def step(index, carry):
            total1, total2 = carry
            part = pl.ds(pl.multiple_of(row + index * 16, 16), 16)
            score = dots[part, cols] * slope
            mass1 = jnp.exp2(score - HIGH_SHIFT)
            mass2 = jnp.exp2(jnp.minimum(score, LOW_CAP) + LOW_SHIFT)
            add1, add2 = mass1[:, :128], mass2[:, :128]
            for lane in range(128, column_count, 128):
                add1 = add1 + mass1[:, lane : lane + 128]
                add2 = add2 + mass2[:, lane : lane + 128]
            row1[part, :] += add1
            row2[part, :] += add2
            return (total1 + mass1[:8] + mass1[8:], total2 + mass2[:8] + mass2[8:])

        zero = jnp.zeros((8, column_count), F32)
        total1, total2 = lax.fori_loop(0, row_count // 16, step, (zero, zero))
        col1[:, cols] += total1
        col2[:, cols] += total2

    def wait_img(*names):
        for name in names:
            copies.arrived("i" + name)

    def wait_txt(place, *names):
        for name in names:
            copies.arrived("t" + name)
            to_core(place, "ab".index(name[-1]))

    def wait_core(*places):
        for place in places:
            copies.arrived("c%d0" % place)
            copies.arrived("c%d1" % place)

    def pass_on(side, name, r, q, place, part, sends):
        wait = wait_img if side[0] == "i" else (lambda n: wait_txt(place, n))
        wait(name + "ab"[part])
        for sent in sends:
            push(side, sent[0], place, part, sent[1], sent[2], sent[3])

    for side in sides:
        pass_on(side, "up", 3, 0, PLACE[3, 0], 0, [("up2", PLACE[2, 0], 1, 0)])
        pass_on(side, "down", 1, 0, PLACE[1, 0], 1, [("down2", PLACE[2, 0], 3, 0)])
    for part in range(2):
        for side in sides:
            pass_on(
                side,
                "z",
                0,
                1,
                PLACE[0, 1],
                part,
                [("zup", PLACE[3, 1], 1, 0), ("zdown", PLACE[1, 1], 3, 0)],
            )
    for side in sides:
        pass_on(side, "up", 3, 0, PLACE[3, 0], 1, [])
        pass_on(side, "down", 1, 0, PLACE[1, 0], 0, [])
    forward(0, 512, 0, 512)
    for side in sides:
        pass_on(side, "up2", 2, 0, PLACE[2, 0], 0, [("up2z", PLACE[2, 1], 0, 1)])
        pass_on(side, "down2", 2, 0, PLACE[2, 0], 1, [("down2z", PLACE[2, 1], 0, 1)])
    wait_core(0, 1, 2, 3)
    forward(0, 512, 1024, 512)
    for part in range(2):
        for side in sides:
            pass_on(side, "zup", 3, 1, PLACE[3, 1], part, [])
            pass_on(side, "zdown", 1, 1, PLACE[1, 1], part, [])
    forward(512, 256, 0, 512)
    forward(0, 768, 512, 256)
    for side in sides:
        pass_on(side, "up2z", 2, 1, PLACE[2, 1], 0, [])
        pass_on(side, "down2z", 2, 1, PLACE[2, 1], 1, [])
    wait_core(4, 5)
    forward(512, 256, 1024, 512)
    forward(0, 768, 1536, 256)
    forward(768, 256, 0, 1024)
    forward(0, 768, 768, 256)
    wait_core(6, 7)
    forward(768, 256, 1024, 1024)
    forward(0, 768, 1792, 256)

    def img_order(r, q):
        return mod4(y + r) * 2 + (1 - odd if q else odd)

    def txt_order(r, q, c):
        return (mod4(x + r) * 2 + (odd if q else 1 - odd)) * 2 + (1 - core if c else core)

    for (r, q), place in PLACE.items():
        rows = pl.ds(place * BLOCK, BLOCK)
        where = img_order(r, q)
        img_stats[0, pl.ds(where, 1), :] = jnp.sum(row1[rows, :].T, axis=0, keepdims=True)
        img_stats[0, pl.ds(8 + where, 1), :] = jnp.sum(row2[rows, :].T, axis=0, keepdims=True)
    for r, q in img_offsets:
        index = PLACE[(4 - r) % 4, q]
        copies.start("si%d" % index, img_stats.at[0], img_stats.at[index], img_peer(r, q))
    for (r, q), place in PLACE.items():
        for c in range(2):
            cols = pl.ds((8 * c + place) * BLOCK, BLOCK)
            where = txt_order(r, q, c)
            txt_stats[0, pl.ds(where, 1), :] = jnp.sum(col1[:, cols], axis=0, keepdims=True)
            txt_stats[0, pl.ds(16 + where, 1), :] = jnp.sum(col2[:, cols], axis=0, keepdims=True)
    for r, q, c in txt_offsets:
        index = 8 * c + PLACE[(4 - r) % 4, q]
        copies.start("st%d" % index, txt_stats.at[0], txt_stats.at[index], txt_peer(r, q, c))

    def log_sum(high, low):
        return jnp.where(
            high >= HIGH_LEAST,
            jnp.log(high) * LOG2E + HIGH_SHIFT,
            jnp.log(jnp.maximum(low, 1e-37)) * LOG2E - LOW_SHIFT,
        )

    img_total = img_stats[0]
    for index in range(1, 8):
        copies.arrived("si%d" % index)
        img_total = img_total + img_stats[index]
    row_lse = log_sum(img_total[:8], img_total[8:])
    row1[0:8, :] = row_lse
    own_lse = row1[pl.ds(img_order(0, 0), 1), :]
    for (r, q), place in PLACE.items():
        one = row1[pl.ds(img_order(r, q), 1), :]
        row_shift[pl.ds(place * BLOCK, BLOCK), :] = jnp.broadcast_to(one + 1.0, (BLOCK, BLOCK)).T
    txt_total = txt_stats[0]
    for index in range(1, 16):
        copies.arrived("st%d" % index)
        txt_total = txt_total + txt_stats[index]
    col_lse = log_sum(txt_total[:16], txt_total[16:])
    row2[0:16, :] = col_lse
    own_lse = own_lse + row2[pl.ds(txt_order(0, 0, 0), 1), :]
    for (r, q), place in PLACE.items():
        for c in range(2):
            one = row2[pl.ds(txt_order(r, q, c), 1), :]
            col_shift[:, pl.ds((8 * c + place) * BLOCK, BLOCK)] = one + 1.0

    def img_id(r, q):
        return img_index * 16 + mod4(y + r) * 4 + (z_img if q else z)

    def txt_id(r, q, c):
        peer = txt_peer(r, q, c)
        return peer[1] * 8 + peer[0]

    txt_ids = [None] * 16
    for (r, q), place in PLACE.items():
        for c in range(2):
            txt_ids[8 * c + place] = txt_id(r, q, c)
    temp_sum = jnp.zeros((8, 128), F32)
    diag_sum = jnp.zeros((8, 128), F32)
    tilt = lax.broadcasted_iota(jnp.int32, (16, 128), 1) - lax.broadcasted_iota(jnp.int32, (16, 128), 0)
    for (r, q), place in PLACE.items():
        this_id = img_id(r, q)

        def weigh(index, carry, this_id=this_id, place=place):
            temp_sum, diag_sum = carry
            part = pl.ds(pl.multiple_of(place * BLOCK + index * 16, 16), 16)
            shift = row_shift[part, :]
            for block in range(16):
                cols = pl.ds(block * BLOCK, BLOCK)
                score = dots[part, cols] * slope
                weight = jnp.exp2(score - shift) + jnp.exp2(score - col_shift[:, cols])
                mask = tilt == (this_id - txt_ids[block]) * BLOCK + index * 16
                weight = jnp.where(mask, weight - 1.0, weight)
                hit = jnp.where(mask, score, 0.0)
                heat = weight * score
                temp_sum = temp_sum + heat[:8] + heat[8:]
                diag_sum = diag_sum + hit[:8] + hit[8:]
                wts[part, cols] = weight.astype(BF16)
            return (temp_sum, diag_sum)

        temp_sum, diag_sum = lax.fori_loop(0, BLOCK // 16, weigh, (temp_sum, diag_sum))
    sums_a[0, 0:1, :] = own_lse - 2.0 * jnp.sum(diag_sum, axis=0, keepdims=True)
    sums_a[0, 1:2, :] = jnp.sum(temp_sum, axis=0, keepdims=True)
    sums_a[0, 2:8, :] = jnp.zeros((6, 128), F32)
    for r, q in img_offsets:
        index = PLACE[(4 - r) % 4, q]
        copies.start("ai%d" % index, sums_a.at[0], sums_a.at[index], img_peer(r, q))

    def image_term(group):
        rows = pl.ds(group * GROUP, GROUP)
        return jnp.dot(wts[rows, :], txt[...], preferred_element_type=F32)

    def text_term(group):
        return lax.dot_general(
            wts[:, pl.ds(group * GROUP, GROUP)],
            img[...],
            (((0,), (0,)), ((), ())),
            preferred_element_type=F32,
        )

    def block(place):
        return pl.ds(place * BLOCK, BLOCK)

    def core_step(group):
        rows = pl.ds(group * GROUP, GROUP)
        core_out[rows, :] = text_term(4 + group).astype(BF16)
        copies.start("k%d" % group, core_out.at[rows], core_in.at[rows], txt_peer(0, 0, 1))

    def group_step(side, group):
        rows = pl.ds(group * GROUP, GROUP)
        if side[0] == "i":
            img_acc[rows, :] = image_term(group)
        else:
            txt_acc[rows, :] = text_term(group)
            copies.arrived("k%d" % group)
            txt_acc[rows, :] += core_in[rows, :].astype(F32)

    trees = (("i", img_acc, img_out, img_in, img_peer), ("t", txt_acc, txt_out, txt_in, txt_peer))

    def give(tree, name, rows, slot, r, q):
        label, acc, out, landing, peer = tree
        out[rows, :] = acc[rows, :].astype(BF16)
        copies.start(label + name, out.at[rows], landing.at[slot], peer(r, q))

    def take(tree, name, rows, slot):
        label, acc, out, landing, peer = tree
        copies.arrived(label + name)
        acc[rows, :] += landing[slot, :].astype(F32)

    for group in (3, 2, 1, 0):
        core_step(group)
        for side, tree in zip(sides, trees):
            group_step(side, group)
            if group == 3:
                give(tree, "far", block(7), block(0), 0, 1)
            if group == 2:
                give(tree, "zup_g", block(4), block(1), 1, 0)
                give(tree, "zdown_g", block(5), block(2), 3, 0)
        if group == 2:
            for tree in trees:
                take(tree, "far", block(6), block(0))
                give(tree, "down2_g", half(6, 0), half(3, 0), 3, 0)
                give(tree, "up2_g", half(6, 1), half(3, 1), 1, 0)
        if group == 1:
            for index in range(1, 8):
                copies.arrived("ai%d" % index)
            total = sums_a[0]
            for index in range(1, 8):
                total = total + sums_a[index]
            sums_b[0] = total
            for r, q, c in txt_offsets:
                index = 8 * c + PLACE[(4 - r) % 4, q]
                copies.start("at%d" % index, sums_b.at[0], sums_b.at[index], txt_peer(r, q, c))
            for tree in trees:
                take(tree, "down2_g", half(3, 0), half(3, 0))
                take(tree, "up2_g", half(2, 1), half(3, 1))
                give(tree, "up_g", block(2), block(4), 1, 0)
                give(tree, "down_g", block(3), block(5), 3, 0)
    for tree in trees:
        take(tree, "zup_g", block(1), block(1))
        take(tree, "zdown_g", block(1), block(2))
        give(tree, "z_g", block(1), block(6), 0, 1)
    for index in range(1, 16):
        copies.arrived("at%d" % index)
    total = sums_b[0]
    for index in range(1, 16):
        total = total + sums_b[index]
    scalars_ref[...] = jnp.broadcast_to(jnp.sum(total, axis=1, keepdims=True), (8, 128))
    for tree, source, out_ref in zip(trees, (image_ref, text_ref), (grad_image_ref, grad_text_ref)):
        label, acc, out, landing, peer = tree
        copies.arrived(label + "up_g")
        copies.arrived(label + "down_g")
        copies.arrived(label + "z_g")

        def finalize(index, carry, source=source, acc=acc, landing=landing, out_ref=out_ref):
            part = pl.ds(pl.multiple_of(index * 16, 16), 16)
            grad = acc[part, :]
            for slot in (4, 5, 6):
                grad = grad + landing[pl.ds(pl.multiple_of(slot * BLOCK + index * 16, 16), 16), :].astype(F32)
            grad = grad * scale
            rows = source[part, :]
            inverse = inverse_of(rows)
            unit = rows * inverse
            out_ref[part, :] = inverse * (grad - unit * jnp.sum(unit * grad, axis=1, keepdims=True))
            return carry

        lax.fori_loop(0, BLOCK // 16, finalize, 0)
    copies.finish()


def on_device(image_feat, text_feat, logit_temp):
    logit_scale = jnp.exp(logit_temp).reshape(1, 1)
    vmem = pl.BlockSpec(memory_space=pltpu.VMEM)
    shape = jax.ShapeDtypeStruct((BLOCK, WIDTH), F32)
    grad_image, grad_text, scalars = pl.pallas_call(
        kernel,
        out_shape=(shape, shape, jax.ShapeDtypeStruct((8, 128), F32)),
        in_specs=[pl.BlockSpec(memory_space=pltpu.SMEM), vmem, vmem],
        out_specs=(vmem, vmem, vmem),
        scratch_shapes=[
            pltpu.VMEM((1024, WIDTH), BF16),
            pltpu.VMEM((2048, WIDTH), BF16),
            pltpu.VMEM((1024, 2048), F32),
            pltpu.VMEM((1024, 2048), BF16),
            pltpu.VMEM((1024, 128), F32),
            pltpu.VMEM((1024, 128), F32),
            pltpu.VMEM((8, 2048), F32),
            pltpu.VMEM((8, 2048), F32),
            pltpu.VMEM((1024, 128), F32),
            pltpu.VMEM((1, 2048), F32),
            pltpu.VMEM((8, 16, 128), F32),
            pltpu.VMEM((16, 32, 128), F32),
            pltpu.VMEM((8, 8, 128), F32),
            pltpu.VMEM((16, 8, 128), F32),
            pltpu.VMEM((1024, WIDTH), F32),
            pltpu.VMEM((1024, WIDTH), F32),
            pltpu.VMEM((1024, WIDTH), BF16),
            pltpu.VMEM((1024, WIDTH), BF16),
            pltpu.VMEM((1024, WIDTH), BF16),
            pltpu.VMEM((7 * BLOCK, WIDTH), BF16),
            pltpu.VMEM((7 * BLOCK, WIDTH), BF16),
            pltpu.VMEM((1024, WIDTH), BF16),
            pltpu.SemaphoreType.DMA((112,)),
            pltpu.SemaphoreType.DMA((112,)),
        ],
        compiler_params=pltpu.CompilerParams(
            collective_id=0, has_side_effects=True, vmem_limit_bytes=60 * 2**20
        ),
        cost_estimate=pl.CostEstimate(flops=16106127360, bytes_accessed=2621440, transcendentals=8388608),
    )(logit_scale, image_feat, text_feat)
    pairs = 16384
    return (
        scalars[0, 0] * (LN2 / (2.0 * pairs)),
        grad_image,
        grad_text,
        scalars[1, 0] * (LN2 / pairs),
    )


def solution(mesh):
    in_specs = (P(("img", "txt"), None), P(("txt", "img"), None), P())
    out_specs = (P(), P(("img", "txt"), None), P(("txt", "img"), None), P())
    return jax.shard_map(
        on_device, mesh=mesh, in_specs=in_specs, out_specs=out_specs, check_vma=False
    )
```

```python
import jax
import jax.numpy as jnp
from jax import lax
from jax.experimental import pallas as pl
from jax.experimental.pallas import tpu as pltpu
from jax.sharding import PartitionSpec as P

PLACE = {(0, 0): 0, (0, 1): 1, (1, 0): 2, (3, 0): 3, (1, 1): 4, (3, 1): 5, (2, 0): 6, (2, 1): 7}
BLOCK = 128
HALF = 64
WIDTH = 1280
PAIRS = 16384
GROUP = 256
LOG2E = 1.4426950408889634
LN2 = 0.6931471805599453
HIGH_SHIFT = 33.0
LOW_SHIFT = 86.0
LOW_CAP = 20.0
HIGH_LEAST = 2.0**-62
F32 = jnp.float32
BF16 = jnp.bfloat16


def mod4(v):
    return lax.rem(v + 4, 4)


class Copies:
    def __init__(self, send_sems, recv_sems):
        self.send_sems, self.recv_sems = send_sems, recv_sems
        self.table = {}

    def start(self, name, src, dst, device):
        index = len(self.table)
        copy = pltpu.make_async_remote_copy(
            src_ref=src,
            dst_ref=dst,
            send_sem=self.send_sems.at[index],
            recv_sem=self.recv_sems.at[index],
            device_id=device,
            device_id_type=pl.DeviceIdType.MESH,
        )
        copy.start()
        self.table[name] = copy

    def arrived(self, name):
        self.table[name].wait_recv()

    def finish(self):
        for copy in self.table.values():
            copy.wait_send()


def kernel(
    scale_ref,
    image_hbm,
    text_hbm,
    loss_ref,
    grad_image_hbm,
    grad_text_hbm,
    temp_ref,
    image_ref,
    text_ref,
    img,
    txt,
    dots,
    wts,
    row1,
    row2,
    col1,
    col2,
    row_shift,
    col_shift,
    diagonals,
    extra,
    img_stats,
    txt_stats,
    sums_a,
    sums_b,
    img_acc,
    txt_acc,
    img_out,
    txt_out,
    core_out,
    img_in,
    txt_in,
    core_in,
    send_sems,
    recv_sems,
    local_sems,
):
    img_index = lax.axis_index("img")
    txt_index = lax.axis_index("txt")
    x, core = img_index // 2, lax.rem(img_index, 2)
    y, z = txt_index // 4, lax.rem(txt_index, 4)
    odd = lax.rem(z, 2)
    z_img = z + 1 - 2 * odd
    z_txt = mod4(z - 1 + 2 * odd)

    def img_peer(r, q):
        return (img_index, mod4(y + r) * 4 + (z_img if q else z))

    def txt_peer(r, q, c=0):
        return (
            mod4(x + r) * 2 + (1 - core if c else core),
            y * 4 + (z_txt if q else z),
        )

    img_offsets = [(r, q) for r in range(4) for q in range(2) if (r, q) != (0, 0)]
    txt_offsets = [
        (r, q, c) for r in range(4) for q in range(2) for c in range(2) if (r, q, c) != (0, 0, 0)
    ]
    load_image = pltpu.make_async_copy(image_hbm, image_ref, local_sems.at[0])
    load_text = pltpu.make_async_copy(text_hbm, text_ref, local_sems.at[1])
    load_image.start()
    load_text.start()
    barrier = pltpu.get_barrier_semaphore()
    for offset in img_offsets:
        pl.semaphore_signal(barrier, inc=1, device_id=img_peer(*offset), device_id_type=pl.DeviceIdType.MESH)
    for offset in txt_offsets:
        pl.semaphore_signal(barrier, inc=1, device_id=txt_peer(*offset), device_id_type=pl.DeviceIdType.MESH)

    scale = scale_ref[0, 0]
    slope = scale * LOG2E

    def inverse_of(rows):
        return lax.rsqrt(jnp.sum(rows * rows, axis=1, keepdims=True) + 1e-06)

    def normalize(source, target):
        def step(index, carry):
            part = pl.ds(pl.multiple_of(index * 16, 16), 16)
            rows = source[part, :]
            target[part, :] = (rows * inverse_of(rows)).astype(BF16)
            return carry

        lax.fori_loop(0, BLOCK // 16, step, 0)

    load_image.wait()
    normalize(image_ref, img)
    load_text.wait()
    normalize(text_ref, txt)
    pl.semaphore_wait(barrier, len(img_offsets) + len(txt_offsets))

    copies = Copies(send_sems, recv_sems)

    def half(place, part):
        return pl.ds(place * BLOCK + part * HALF, HALF)

    sides = (("i", img, img_peer), ("t", txt, txt_peer))

    def push(side, name, place, part, to_place, r, q):
        label, rows, peer = side
        copies.start(
            label + name + "ab"[part], rows.at[half(place, part)], rows.at[half(to_place, part)], peer(r, q)
        )

    def to_core(place, part):
        copies.start(
            "c%d%d" % (place, part),
            txt.at[half(place, part)],
            txt.at[half(8 + place, part)],
            txt_peer(0, 0, 1),
        )

    for first in range(2):
        for side in sides:
            push(side, "up", 0, first, PLACE[3, 0], 1, 0)
            push(side, "down", 0, 1 - first, PLACE[1, 0], 3, 0)
            push(side, "z", 0, first, PLACE[0, 1], 0, 1)
        to_core(0, first)

    row1[...] = jnp.zeros_like(row1)
    row2[...] = jnp.zeros_like(row2)
    col1[...] = jnp.zeros_like(col1)
    col2[...] = jnp.zeros_like(col2)

    def forward(row, row_count, column, column_count):
        cols = pl.ds(column, column_count)
        dots[pl.ds(row, row_count), cols] = lax.dot_general(
            img[pl.ds(row, row_count), :],
            txt[cols, :],
            (((1,), (1,)), ((), ())),
            preferred_element_type=F32,
        )

        def step(index, carry):
            part = pl.ds(pl.multiple_of(row + index * 32, 32), 32)
            add1 = jnp.zeros((32, 128), F32)
            add2 = jnp.zeros((32, 128), F32)
            for lane in range(column, column + column_count, 128):
                block_cols = pl.ds(lane, 128)
                score = dots[part, block_cols] * slope
                dots[part, block_cols] = score
                mass1 = jnp.exp2(score - HIGH_SHIFT)
                mass2 = jnp.exp2(jnp.minimum(score, LOW_CAP) + LOW_SHIFT)
                add1 = add1 + mass1
                add2 = add2 + mass2
                col1[:, block_cols] += (mass1[:8] + mass1[8:16]) + (mass1[16:24] + mass1[24:])
                col2[:, block_cols] += (mass2[:8] + mass2[8:16]) + (mass2[16:24] + mass2[24:])
            row1[part, :] += add1
            row2[part, :] += add2
            return carry

        lax.fori_loop(0, row_count // 32, step, 0)

    def wait_img(*names):
        for name in names:
            copies.arrived("i" + name)

    def wait_txt(place, *names):
        for name in names:
            copies.arrived("t" + name)
            to_core(place, "ab".index(name[-1]))

    def wait_core(*places):
        for place in places:
            copies.arrived("c%d0" % place)
            copies.arrived("c%d1" % place)

    def pass_on(side, name, r, q, place, part, sends):
        wait = wait_img if side[0] == "i" else (lambda n: wait_txt(place, n))
        wait(name + "ab"[part])
        for sent in sends:
            push(side, sent[0], place, part, sent[1], sent[2], sent[3])

    for side in sides:
        pass_on(side, "up", 3, 0, PLACE[3, 0], 0, [("up2", PLACE[2, 0], 1, 0)])
        pass_on(side, "down", 1, 0, PLACE[1, 0], 1, [("down2", PLACE[2, 0], 3, 0)])
    for part in range(2):
        for side in sides:
            pass_on(
                side,
                "z",
                0,
                1,
                PLACE[0, 1],
                part,
                [("zup", PLACE[3, 1], 1, 0), ("zdown", PLACE[1, 1], 3, 0)],
            )
    for side in sides:
        pass_on(side, "up", 3, 0, PLACE[3, 0], 1, [])
        pass_on(side, "down", 1, 0, PLACE[1, 0], 0, [])
    forward(0, 512, 0, 512)
    for side in sides:
        pass_on(side, "up2", 2, 0, PLACE[2, 0], 0, [("up2z", PLACE[2, 1], 0, 1)])
        pass_on(side, "down2", 2, 0, PLACE[2, 0], 1, [("down2z", PLACE[2, 1], 0, 1)])
    wait_core(0, 1, 2, 3)
    forward(0, 512, 1024, 512)
    for part in range(2):
        for side in sides:
            pass_on(side, "zup", 3, 1, PLACE[3, 1], part, [])
            pass_on(side, "zdown", 1, 1, PLACE[1, 1], part, [])
    forward(512, 256, 0, 512)
    forward(0, 768, 512, 256)
    for side in sides:
        pass_on(side, "up2z", 2, 1, PLACE[2, 1], 0, [])
        pass_on(side, "down2z", 2, 1, PLACE[2, 1], 1, [])
    wait_core(4, 5)
    forward(512, 256, 1024, 512)
    forward(0, 768, 1536, 256)
    forward(768, 256, 0, 1024)
    forward(0, 768, 768, 256)
    wait_core(6, 7)
    forward(768, 256, 1024, 1024)
    forward(0, 768, 1792, 256)

    def img_order(r, q):
        return mod4(y + r) * 2 + (1 - odd if q else odd)

    def txt_order(r, q, c):
        return (mod4(x + r) * 2 + (odd if q else 1 - odd)) * 2 + (1 - core if c else core)

    for (r, q), place in PLACE.items():
        rows = pl.ds(place * BLOCK, BLOCK)
        where = img_order(r, q)
        img_stats[0, pl.ds(where, 1), :] = jnp.sum(row1[rows, :].T, axis=0, keepdims=True)
        img_stats[0, pl.ds(8 + where, 1), :] = jnp.sum(row2[rows, :].T, axis=0, keepdims=True)
    for r, q in img_offsets:
        index = PLACE[(4 - r) % 4, q]
        copies.start("si%d" % index, img_stats.at[0], img_stats.at[index], img_peer(r, q))
    for (r, q), place in PLACE.items():
        for c in range(2):
            cols = pl.ds((8 * c + place) * BLOCK, BLOCK)
            where = txt_order(r, q, c)
            txt_stats[0, pl.ds(where, 1), :] = jnp.sum(col1[:, cols], axis=0, keepdims=True)
            txt_stats[0, pl.ds(16 + where, 1), :] = jnp.sum(col2[:, cols], axis=0, keepdims=True)
    for r, q, c in txt_offsets:
        index = 8 * c + PLACE[(4 - r) % 4, q]
        copies.start("st%d" % index, txt_stats.at[0], txt_stats.at[index], txt_peer(r, q, c))

    eye = lax.broadcasted_iota(jnp.int32, (BLOCK, BLOCK), 0) == lax.broadcasted_iota(jnp.int32, (BLOCK, BLOCK), 1)

    def on_diagonal(place, body):
        r, q = [key for key in PLACE if PLACE[key] == place][0]
        y_row, z_row = mod4(y + r), (z_img if q else z)
        x_text, z_text, core_text = lax.rem(y_row, 2) * 2 + z_row // 2, 2 * core + y_row // 2, lax.rem(z_row, 2)
        near = jnp.where(z_text == z, 1, 0)
        far = jnp.where(z_text == z_txt, 1, 0)
        ring = mod4(x_text - x)
        place_text = jnp.where(
            ring == 0, far, jnp.where(ring == 1, 2 + 2 * far, jnp.where(ring == 2, 6 + far, 3 + 2 * far))
        )
        place_text = place_text + 8 * jnp.where(core_text == core, 0, 1)

        @pl.when(jnp.where(x == y, near + far, 0) == 1)
        def _():
            body(pl.ds(place * BLOCK, BLOCK), pl.ds(pl.multiple_of(place_text * BLOCK, BLOCK), BLOCK))

    for place in range(8):

        def set_aside(rows, cols, place=place):
            scores = dots[rows, cols]
            diagonals[place] = scores
            dots[rows, cols] = jnp.where(eye, -10000.0, scores)

        on_diagonal(place, set_aside)

    def log_sum(high, low):
        return jnp.where(
            high >= HIGH_LEAST,
            jnp.log(high) * LOG2E + HIGH_SHIFT,
            jnp.log(jnp.maximum(low, 1e-37)) * LOG2E - LOW_SHIFT,
        )

    img_total = img_stats[0]
    for index in range(1, 8):
        copies.arrived("si%d" % index)
        img_total = img_total + img_stats[index]
    row_lse = log_sum(img_total[:8], img_total[8:])
    row1[0:8, :] = row_lse
    own_lse = row1[pl.ds(img_order(0, 0), 1), :]
    for (r, q), place in PLACE.items():
        one = row1[pl.ds(img_order(r, q), 1), :]
        row_shift[pl.ds(place * BLOCK, BLOCK), :] = jnp.broadcast_to(one + 1.0, (BLOCK, BLOCK)).T
    txt_total = txt_stats[0]
    for index in range(1, 16):
        copies.arrived("st%d" % index)
        txt_total = txt_total + txt_stats[index]
    col_lse = log_sum(txt_total[:16], txt_total[16:])
    row2[0:16, :] = col_lse
    own_lse = own_lse + row2[pl.ds(txt_order(0, 0, 0), 1), :]
    for (r, q), place in PLACE.items():
        for c in range(2):
            one = row2[pl.ds(txt_order(r, q, c), 1), :]
            col_shift[:, pl.ds((8 * c + place) * BLOCK, BLOCK)] = one + 1.0

    extra[...] = jnp.zeros_like(extra)
    heat = jnp.zeros((16, 128), F32)
    for place in (7, 4, 5, 6, 1, 2, 3, 0):

        def weigh(index, heat, place=place):
            part = pl.ds(pl.multiple_of(place * BLOCK + index * 16, 16), 16)
            shift = row_shift[part, :]
            for block in range(16):
                cols = pl.ds(block * BLOCK, BLOCK)
                score = dots[part, cols]
                weight = jnp.exp2(score - shift) + jnp.exp2(score - col_shift[:, cols])
                heat = heat + weight * score
                wts[part, cols] = weight.astype(BF16)
            return heat

        heat = lax.fori_loop(0, BLOCK // 16, weigh, heat)

        def put_back(rows, cols, place=place):
            scores = diagonals[place]
            weight = jnp.exp2(scores - row_shift[rows, :]) + jnp.exp2(scores - col_shift[:, cols])
            weight = jnp.where(eye, weight - 1.0, weight)
            wts[rows, cols] = weight.astype(BF16)
            extra[0:1, :] += jnp.sum(jnp.where(eye, scores, 0.0), axis=0, keepdims=True)
            extra[1:2, :] += jnp.sum(jnp.where(eye, weight * scores, 0.0), axis=0, keepdims=True)

        on_diagonal(place, put_back)
    sums_a[0, 0:1, :] = own_lse - 2.0 * extra[0:1, :]
    sums_a[0, 1:2, :] = jnp.sum(heat, axis=0, keepdims=True) + extra[1:2, :]
    sums_a[0, 2:8, :] = jnp.zeros((6, 128), F32)
    for r, q in img_offsets:
        index = PLACE[(4 - r) % 4, q]
        copies.start("ai%d" % index, sums_a.at[0], sums_a.at[index], img_peer(r, q))

    def block(place):
        return pl.ds(place * BLOCK, BLOCK)

    def rows_of(group):
        return pl.ds(group * GROUP, GROUP)

    def image_term(group):
        return jnp.dot(wts[rows_of(group), :], txt[...], preferred_element_type=F32)

    def text_term(group):
        return lax.dot_general(
            wts[:, rows_of(group)], img[...], (((0,), (0,)), ((), ())), preferred_element_type=F32
        )

    def core_step(group):
        rows = rows_of(group)
        core_out[rows, :] = text_term(4 + group).astype(BF16)
        copies.start("k%d" % group, core_out.at[rows], core_in.at[rows], txt_peer(0, 0, 1))

    def text_group(group):
        term = text_term(group)
        copies.arrived("k%d" % group)
        return term + core_in[rows_of(group), :].astype(F32)

    trees = (("i", img_acc, img_out, img_in, img_peer), ("t", txt_acc, txt_out, txt_in, txt_peer))

    def hold(tree, group):
        tree[1][rows_of(group), :] = image_term(group) if tree[0] == "i" else text_group(group)

    def hold_low(tree, group):
        term = image_term(group) if tree[0] == "i" else text_group(group)
        tree[2][rows_of(group), :] = term.astype(BF16)

    def send(tree, name, place, first, count, to_place, r, q):
        label, acc, out, landing, peer = tree
        rows = pl.ds(place * BLOCK + first, count)
        copies.start(label + name, out.at[rows], landing.at[pl.ds(to_place * BLOCK + first, count)], peer(r, q))

    def lower(tree, place, first, count, slots=()):
        label, acc, out, landing, peer = tree

        def step(index, carry):
            at = place * BLOCK + first + index * 16
            rows = pl.ds(pl.multiple_of(at, 16), 16)
            total = acc[rows, :]
            for slot in slots:
                at = slot * BLOCK + first + index * 16
                total = total + landing[pl.ds(pl.multiple_of(at, 16), 16), :].astype(F32)
            out[rows, :] = total.astype(BF16)
            return carry

        lax.fori_loop(0, count // 16, step, 0)

    def far_step(tree):
        hold(tree, 3)
        for first, name in ((0, "far_a"), (HALF, "far_b")):
            lower(tree, 7, first, HALF)
            send(tree, name, 7, first, HALF, 0, 0, 1)

    def ring_step(tree):
        hold_low(tree, 2)
        for part, name in ((0, "a"), (HALF, "b")):
            send(tree, "zup_" + name, 4, part, HALF, 1, 1, 0)
            send(tree, "zdown_" + name, 5, part, HALF, 2, 3, 0)

    def turn_step(tree):
        copies.arrived(tree[0] + "far_a")
        lower(tree, 6, 0, HALF, (0,))
        send(tree, "down2_g", 6, 0, HALF, 3, 3, 0)
        copies.arrived(tree[0] + "far_b")
        lower(tree, 6, HALF, HALF, (0,))
        send(tree, "up2_g", 6, HALF, HALF, 3, 1, 0)

    def free_step(tree):
        hold(tree, 1)
        lower(tree, 2, 0, HALF)
        send(tree, "up_free", 2, 0, HALF, 4, 1, 0)
        lower(tree, 3, HALF, HALF)
        send(tree, "down_free", 3, HALF, HALF, 5, 3, 0)

    def pair_step(tree):
        for first, name in ((0, "a"), (HALF, "b")):
            copies.arrived(tree[0] + "zup_" + name)
            copies.arrived(tree[0] + "zdown_" + name)
            lower(tree, 1, first, HALF, (1, 2))
            send(tree, "z_" + name, 1, first, HALF, 6, 0, 1)

    def last_step(tree):
        copies.arrived(tree[0] + "up2_g")
        lower(tree, 2, HALF, HALF, (3,))
        send(tree, "up_last", 2, HALF, HALF, 4, 1, 0)
        copies.arrived(tree[0] + "down2_g")
        lower(tree, 3, 0, HALF, (3,))
        send(tree, "down_last", 3, 0, HALF, 5, 3, 0)

    image_tree, text_tree = trees
    core_step(3)
    core_step(2)
    far_step(text_tree)
    ring_step(text_tree)
    far_step(image_tree)
    ring_step(image_tree)
    core_step(1)
    core_step(0)
    turn_step(text_tree)
    free_step(text_tree)
    turn_step(image_tree)
    free_step(image_tree)
    for index in range(1, 8):
        copies.arrived("ai%d" % index)
    total = sums_a[0]
    for index in range(1, 8):
        total = total + sums_a[index]
    sums_b[0] = total
    for r, q, c in txt_offsets:
        index = 8 * c + PLACE[(4 - r) % 4, q]
        copies.start("at%d" % index, sums_b.at[0], sums_b.at[index], txt_peer(r, q, c))
    hold(text_tree, 0)
    pair_step(text_tree)
    last_step(text_tree)
    hold(image_tree, 0)
    pair_step(image_tree)
    last_step(image_tree)
    for index in range(1, 16):
        copies.arrived("at%d" % index)
    total = sums_b[0]
    for index in range(1, 16):
        total = total + sums_b[index]
    loss_ref[0, 0] = jnp.sum(total[0:1, :]) * (LN2 / (2.0 * PAIRS))
    temp_ref[0, 0] = jnp.sum(total[1:2, :]) * (LN2 / PAIRS)
    stores = []
    results = ((text_tree, text_ref, grad_text_hbm), (image_tree, image_ref, grad_image_hbm))
    for tree, source, result in results:
        label, acc, out, landing, peer = tree
        for name in ("up_free", "down_free", "z_a", "z_b", "up_last", "down_last"):
            copies.arrived(label + name)

        def finalize(index, carry, source=source, acc=acc, landing=landing):
            part = pl.ds(pl.multiple_of(index * 16, 16), 16)
            grad = acc[part, :]
            for slot in (4, 5, 6):
                grad = grad + landing[pl.ds(pl.multiple_of(slot * BLOCK + index * 16, 16), 16), :].astype(F32)
            grad = grad * scale
            rows = source[part, :]
            inverse = inverse_of(rows)
            unit = rows * inverse
            source[part, :] = inverse * (grad - unit * jnp.sum(unit * grad, axis=1, keepdims=True))
            return carry

        lax.fori_loop(0, BLOCK // 16, finalize, 0)
        stores.append(pltpu.make_async_copy(source, result, local_sems.at[2 + len(stores)]))
        stores[-1].start()
    copies.finish()
    for store in stores:
        store.wait()


def on_device(image_feat, text_feat, logit_temp):
    logit_scale = jnp.exp(logit_temp).reshape(1, 1)
    smem = pl.BlockSpec(memory_space=pltpu.SMEM)
    anywhere = pl.BlockSpec(memory_space=pl.ANY)
    one = jax.ShapeDtypeStruct((1, 1), F32)
    shape = jax.ShapeDtypeStruct((BLOCK, WIDTH), F32)
    mean_loss, grad_image, grad_text, temp_grad = pl.pallas_call(
        kernel,
        out_shape=(one, shape, shape, one),
        in_specs=[smem, anywhere, anywhere],
        out_specs=(smem, anywhere, anywhere, smem),
        scratch_shapes=[
            pltpu.VMEM((BLOCK, WIDTH), F32),
            pltpu.VMEM((BLOCK, WIDTH), F32),
            pltpu.VMEM((1024, WIDTH), BF16),
            pltpu.VMEM((2048, WIDTH), BF16),
            pltpu.VMEM((1024, 2048), F32),
            pltpu.VMEM((1024, 2048), BF16),
            pltpu.VMEM((1024, 128), F32),
            pltpu.VMEM((1024, 128), F32),
            pltpu.VMEM((8, 2048), F32),
            pltpu.VMEM((8, 2048), F32),
            pltpu.VMEM((1024, 128), F32),
            pltpu.VMEM((1, 2048), F32),
            pltpu.VMEM((8, BLOCK, BLOCK), F32),
            pltpu.VMEM((8, 128), F32),
            pltpu.VMEM((8, 16, 128), F32),
            pltpu.VMEM((16, 32, 128), F32),
            pltpu.VMEM((8, 8, 128), F32),
            pltpu.VMEM((16, 8, 128), F32),
            pltpu.VMEM((1024, WIDTH), F32),
            pltpu.VMEM((1024, WIDTH), F32),
            pltpu.VMEM((1024, WIDTH), BF16),
            pltpu.VMEM((1024, WIDTH), BF16),
            pltpu.VMEM((1024, WIDTH), BF16),
            pltpu.VMEM((7 * BLOCK, WIDTH), BF16),
            pltpu.VMEM((7 * BLOCK, WIDTH), BF16),
            pltpu.VMEM((1024, WIDTH), BF16),
            pltpu.SemaphoreType.DMA((128,)),
            pltpu.SemaphoreType.DMA((128,)),
            pltpu.SemaphoreType.DMA((4,)),
        ],
        compiler_params=pltpu.CompilerParams(
            collective_id=0, has_side_effects=True, vmem_limit_bytes=60 * 2**20
        ),
        cost_estimate=pl.CostEstimate(flops=16106127360, bytes_accessed=2621440, transcendentals=8388608),
    )(logit_scale, image_feat, text_feat)
    return (mean_loss[0, 0], grad_image, grad_text, temp_grad[0, 0])


def solution(mesh):
    in_specs = (P(("img", "txt"), None), P(("txt", "img"), None), P())
    out_specs = (P(), P(("img", "txt"), None), P(("txt", "img"), None), P())
    return jax.shard_map(
        on_device, mesh=mesh, in_specs=in_specs, out_specs=out_specs, check_vma=False
    )
```

```python
import functools

import jax
import jax.numpy as jnp
from jax import lax
from jax.experimental import pallas as pl
from jax.experimental.pallas import tpu as pltpu
from jax.sharding import PartitionSpec as P

PLACE = {(0, 0): 0, (0, 1): 1, (1, 0): 2, (3, 0): 3, (1, 1): 4, (3, 1): 5, (2, 0): 6, (2, 1): 7}
BLOCK = 128
HALF = 64
WIDTH = 1280
PAIRS = 16384
GROUP = 256
LOG2E = 1.4426950408889634
LN2 = 0.6931471805599453
HIGH_SHIFT = 33.0
LOW_SHIFT = 86.0
LOW_CAP = 20.0
HIGH_LEAST = 2.0**-62
F32 = jnp.float32
BF16 = jnp.bfloat16


def mod4(v):
    return lax.rem(v + 4, 4)


class Copies:
    def __init__(self, send_sems, recv_sems):
        self.send_sems, self.recv_sems = send_sems, recv_sems
        self.table = {}

    def start(self, name, src, dst, device):
        index = len(self.table)
        copy = pltpu.make_async_remote_copy(
            src_ref=src,
            dst_ref=dst,
            send_sem=self.send_sems.at[index],
            recv_sem=self.recv_sems.at[index],
            device_id=device,
            device_id_type=pl.DeviceIdType.MESH,
        )
        copy.start()
        self.table[name] = copy

    def arrived(self, name):
        self.table[name].wait_recv()

    def finish(self):
        for copy in self.table.values():
            copy.wait_send()


def kernel(
    scale_ref,
    image_hbm,
    text_hbm,
    loss_ref,
    grad_image_hbm,
    grad_text_hbm,
    temp_ref,
    image_ref,
    text_ref,
    img,
    txt,
    dots,
    wts,
    row1,
    row2,
    col1,
    col2,
    row_shift,
    col_shift,
    diagonals,
    extra,
    img_stats,
    txt_stats,
    sums_a,
    sums_b,
    img_acc,
    txt_acc,
    img_out,
    txt_out,
    core_out,
    img_in,
    txt_in,
    core_in,
    send_sems,
    recv_sems,
    local_sems,
):
    img_index = lax.axis_index("img")
    txt_index = lax.axis_index("txt")
    x, core = img_index // 2, lax.rem(img_index, 2)
    y, z = txt_index // 4, lax.rem(txt_index, 4)
    odd = lax.rem(z, 2)
    z_img = z + 1 - 2 * odd
    z_txt = mod4(z - 1 + 2 * odd)

    def img_peer(r, q):
        return (img_index, mod4(y + r) * 4 + (z_img if q else z))

    def txt_peer(r, q, c=0):
        return (
            mod4(x + r) * 2 + (1 - core if c else core),
            y * 4 + (z_txt if q else z),
        )

    img_offsets = [(r, q) for r in range(4) for q in range(2) if (r, q) != (0, 0)]
    txt_offsets = [
        (r, q, c) for r in range(4) for q in range(2) for c in range(2) if (r, q, c) != (0, 0, 0)
    ]
    load_image = pltpu.make_async_copy(image_hbm, image_ref, local_sems.at[0])
    load_text = pltpu.make_async_copy(text_hbm, text_ref, local_sems.at[1])
    load_image.start()
    load_text.start()
    barrier = pltpu.get_barrier_semaphore()
    for offset in img_offsets:
        pl.semaphore_signal(barrier, inc=1, device_id=img_peer(*offset), device_id_type=pl.DeviceIdType.MESH)
    for offset in txt_offsets:
        pl.semaphore_signal(barrier, inc=1, device_id=txt_peer(*offset), device_id_type=pl.DeviceIdType.MESH)

    scale = scale_ref[0, 0]
    slope = scale * LOG2E

    def inverse_of(rows):
        return lax.rsqrt(jnp.sum(rows * rows, axis=1, keepdims=True) + 1e-06)

    def normalize(source, target):
        def step(index, carry):
            part = pl.ds(pl.multiple_of(index * 16, 16), 16)
            rows = source[part, :]
            target[part, :] = (rows * inverse_of(rows)).astype(BF16)
            return carry

        lax.fori_loop(0, BLOCK // 16, step, 0)

    load_image.wait()
    normalize(image_ref, img)
    load_text.wait()
    normalize(text_ref, txt)
    pl.semaphore_wait(barrier, len(img_offsets) + len(txt_offsets))

    copies = Copies(send_sems, recv_sems)

    def half(place, part):
        return pl.ds(place * BLOCK + part * HALF, HALF)

    sides = (("i", img, img_peer), ("t", txt, txt_peer))

    def push(side, name, place, part, to_place, r, q):
        label, rows, peer = side
        copies.start(
            label + name + "ab"[part], rows.at[half(place, part)], rows.at[half(to_place, part)], peer(r, q)
        )

    def to_core(place, part):
        copies.start(
            "c%d%d" % (place, part),
            txt.at[half(place, part)],
            txt.at[half(8 + place, part)],
            txt_peer(0, 0, 1),
        )

    for first in range(2):
        for side in sides:
            push(side, "up", 0, first, PLACE[3, 0], 1, 0)
            push(side, "down", 0, 1 - first, PLACE[1, 0], 3, 0)
            push(side, "z", 0, first, PLACE[0, 1], 0, 1)
        to_core(0, first)

    row1[...] = jnp.zeros_like(row1)
    row2[...] = jnp.zeros_like(row2)
    col1[...] = jnp.zeros_like(col1)
    col2[...] = jnp.zeros_like(col2)

    def forward(row, row_count, column, column_count):
        cols = pl.ds(column, column_count)
        product = lax.dot_general(
            img[pl.ds(row, row_count), :],
            txt[cols, :],
            (((1,), (1,)), ((), ())),
            preferred_element_type=F32,
        )
        dots[pl.ds(row, row_count), cols] = product * slope

        for first in range(row, row + row_count, 32):
            part = pl.ds(first, 32)
            add1 = jnp.zeros((32, 128), F32)
            add2 = jnp.zeros((32, 128), F32)
            for lane in range(column, column + column_count, 128):
                block_cols = pl.ds(lane, 128)
                score = dots[part, block_cols]
                mass1 = jnp.exp2(score - HIGH_SHIFT)
                mass2 = jnp.exp2(jnp.minimum(score, LOW_CAP) + LOW_SHIFT)
                add1 = add1 + mass1
                add2 = add2 + mass2
                col1[:, block_cols] += jnp.sum(mass1.reshape(32 // 8, 8, 128), axis=0)
                col2[:, block_cols] += jnp.sum(mass2.reshape(32 // 8, 8, 128), axis=0)
            row1[part, :] += add1
            row2[part, :] += add2

    def wait_img(*names):
        for name in names:
            copies.arrived("i" + name)

    def wait_txt(place, *names):
        for name in names:
            copies.arrived("t" + name)
            to_core(place, "ab".index(name[-1]))

    def wait_core(*places):
        for place in places:
            copies.arrived("c%d0" % place)
            copies.arrived("c%d1" % place)

    def pass_on(side, name, r, q, place, part, sends):
        wait = wait_img if side[0] == "i" else (lambda n: wait_txt(place, n))
        wait(name + "ab"[part])
        for sent in sends:
            push(side, sent[0], place, part, sent[1], sent[2], sent[3])

    for side in sides:
        pass_on(side, "up", 3, 0, PLACE[3, 0], 0, [("up2", PLACE[2, 0], 1, 0)])
        pass_on(side, "down", 1, 0, PLACE[1, 0], 1, [("down2", PLACE[2, 0], 3, 0)])
    for part in range(2):
        for side in sides:
            pass_on(
                side,
                "z",
                0,
                1,
                PLACE[0, 1],
                part,
                [("zup", PLACE[3, 1], 1, 0), ("zdown", PLACE[1, 1], 3, 0)],
            )
    for side in sides:
        pass_on(side, "up", 3, 0, PLACE[3, 0], 1, [])
        pass_on(side, "down", 1, 0, PLACE[1, 0], 0, [])
    forward(0, 512, 0, 512)
    for side in sides:
        pass_on(side, "up2", 2, 0, PLACE[2, 0], 0, [("up2z", PLACE[2, 1], 0, 1)])
        pass_on(side, "down2", 2, 0, PLACE[2, 0], 1, [("down2z", PLACE[2, 1], 0, 1)])
    wait_core(0, 1, 2, 3)
    forward(0, 512, 1024, 512)
    for part in range(2):
        for side in sides:
            pass_on(side, "zup", 3, 1, PLACE[3, 1], part, [])
            pass_on(side, "zdown", 1, 1, PLACE[1, 1], part, [])
    forward(512, 256, 0, 512)
    forward(0, 768, 512, 256)
    for side in sides:
        pass_on(side, "up2z", 2, 1, PLACE[2, 1], 0, [])
        pass_on(side, "down2z", 2, 1, PLACE[2, 1], 1, [])
    wait_core(4, 5)
    forward(512, 256, 1024, 512)
    forward(0, 768, 1536, 256)
    forward(768, 256, 0, 1024)
    forward(0, 768, 768, 256)
    wait_core(6, 7)
    forward(768, 256, 1024, 1024)
    forward(0, 768, 1792, 256)

    def img_order(r, q):
        return mod4(y + r) * 2 + (1 - odd if q else odd)

    def txt_order(r, q, c):
        return (mod4(x + r) * 2 + (odd if q else 1 - odd)) * 2 + (1 - core if c else core)

    for (r, q), place in PLACE.items():
        rows = pl.ds(place * BLOCK, BLOCK)
        where = img_order(r, q)
        img_stats[0, pl.ds(where, 1), :] = jnp.sum(row1[rows, :].T, axis=0, keepdims=True)
        img_stats[0, pl.ds(8 + where, 1), :] = jnp.sum(row2[rows, :].T, axis=0, keepdims=True)
    for r, q in img_offsets:
        index = PLACE[(4 - r) % 4, q]
        copies.start("si%d" % index, img_stats.at[0], img_stats.at[index], img_peer(r, q))
    for (r, q), place in PLACE.items():
        for c in range(2):
            cols = pl.ds((8 * c + place) * BLOCK, BLOCK)
            where = txt_order(r, q, c)
            txt_stats[0, pl.ds(where, 1), :] = jnp.sum(col1[:, cols], axis=0, keepdims=True)
            txt_stats[0, pl.ds(16 + where, 1), :] = jnp.sum(col2[:, cols], axis=0, keepdims=True)
    for r, q, c in txt_offsets:
        index = 8 * c + PLACE[(4 - r) % 4, q]
        copies.start("st%d" % index, txt_stats.at[0], txt_stats.at[index], txt_peer(r, q, c))

    eye = lax.broadcasted_iota(jnp.int32, (BLOCK, BLOCK), 0) == lax.broadcasted_iota(jnp.int32, (BLOCK, BLOCK), 1)

    def on_diagonal(place, body):
        r, q = [key for key in PLACE if PLACE[key] == place][0]
        y_row, z_row = mod4(y + r), (z_img if q else z)
        x_text, z_text, core_text = lax.rem(y_row, 2) * 2 + z_row // 2, 2 * core + y_row // 2, lax.rem(z_row, 2)
        near = jnp.where(z_text == z, 1, 0)
        far = jnp.where(z_text == z_txt, 1, 0)
        ring = mod4(x_text - x)
        place_text = jnp.where(
            ring == 0, far, jnp.where(ring == 1, 2 + 2 * far, jnp.where(ring == 2, 6 + far, 3 + 2 * far))
        )
        place_text = place_text + 8 * jnp.where(core_text == core, 0, 1)

        @pl.when(jnp.where(x == y, near + far, 0) == 1)
        def _():
            body(pl.ds(place * BLOCK, BLOCK), pl.ds(pl.multiple_of(place_text * BLOCK, BLOCK), BLOCK))

    for place in range(8):

        def set_aside(rows, cols, place=place):
            scores = dots[rows, cols]
            diagonals[place] = scores
            dots[rows, cols] = jnp.where(eye, -10000.0, scores)

        on_diagonal(place, set_aside)

    def log_sum(high, low):
        return jnp.where(
            high >= HIGH_LEAST,
            jnp.log(high) * LOG2E + HIGH_SHIFT,
            jnp.log(jnp.maximum(low, 1e-37)) * LOG2E - LOW_SHIFT,
        )

    img_total = img_stats[0]
    for index in range(1, 8):
        copies.arrived("si%d" % index)
        img_total = img_total + img_stats[index]
    row_lse = log_sum(img_total[:8], img_total[8:])
    row1[0:8, :] = row_lse
    own_lse = row1[pl.ds(img_order(0, 0), 1), :]
    for (r, q), place in PLACE.items():
        one = row1[pl.ds(img_order(r, q), 1), :]
        row_shift[pl.ds(place * BLOCK, BLOCK), :] = jnp.broadcast_to(one + 1.0, (BLOCK, BLOCK)).T
    txt_total = txt_stats[0]
    for index in range(1, 16):
        copies.arrived("st%d" % index)
        txt_total = txt_total + txt_stats[index]
    col_lse = log_sum(txt_total[:16], txt_total[16:])
    row2[0:16, :] = col_lse
    own_lse = own_lse + row2[pl.ds(txt_order(0, 0, 0), 1), :]
    for (r, q), place in PLACE.items():
        for c in range(2):
            one = row2[pl.ds(txt_order(r, q, c), 1), :]
            col_shift[:, pl.ds((8 * c + place) * BLOCK, BLOCK)] = one + 1.0

    extra[...] = jnp.zeros_like(extra)
    heats = [jnp.zeros((16, 128), F32)] * 4

    def weigh(*places):
        for place in places:
            for first in range(place * BLOCK, place * BLOCK + BLOCK, 16):
                part = pl.ds(first, 16)
                shift = row_shift[part, :]
                for block in range(16):
                    cols = pl.ds(block * BLOCK, BLOCK)
                    score = dots[part, cols]
                    weight = jnp.exp2(score - shift) + jnp.exp2(score - col_shift[:, cols])
                    heats[block % 4] = heats[block % 4] + weight * score
                    wts[part, cols] = weight.astype(BF16)

    def put_back(*places):
        def body(place, rows, cols):
            scores = diagonals[place]
            weight = jnp.exp2(scores - row_shift[rows, :]) + jnp.exp2(scores - col_shift[:, cols])
            weight = jnp.where(eye, weight - 1.0, weight)
            wts[rows, cols] = weight.astype(BF16)
            extra[0:1, :] += jnp.sum(jnp.where(eye, scores, 0.0), axis=0, keepdims=True)
            extra[1:2, :] += jnp.sum(jnp.where(eye, weight * scores, 0.0), axis=0, keepdims=True)

        for place in places:
            on_diagonal(place, functools.partial(body, place))

    def block(place):
        return pl.ds(place * BLOCK, BLOCK)

    def rows_of(group):
        return pl.ds(group * GROUP, GROUP)

    def image_term(group):
        return jnp.dot(wts[rows_of(group), :], txt[...], preferred_element_type=F32)

    def text_term(group):
        return lax.dot_general(
            wts[:, rows_of(group)], img[...], (((0,), (0,)), ((), ())), preferred_element_type=F32
        )

    def core_step(group):
        rows = rows_of(group)
        core_out[rows, :] = text_term(4 + group).astype(BF16)
        copies.start("k%d" % group, core_out.at[rows], core_in.at[rows], txt_peer(0, 0, 1))

    def text_group(group):
        term = text_term(group)
        copies.arrived("k%d" % group)
        return term + core_in[rows_of(group), :].astype(F32)

    trees = (("i", img_acc, img_out, img_in, img_peer), ("t", txt_acc, txt_out, txt_in, txt_peer))

    def group_term(tree, group):
        return image_term(group) if tree[0] == "i" else text_group(group)

    def send(tree, name, place, first, count, to_place, r, q):
        label, acc, out, landing, peer = tree
        rows = pl.ds(place * BLOCK + first, count)
        copies.start(label + name, out.at[rows], landing.at[pl.ds(to_place * BLOCK + first, count)], peer(r, q))

    def lower(tree, place, first, count, slots):
        label, acc, out, landing, peer = tree
        rows = pl.ds(place * BLOCK + first, count)
        total = acc[rows, :]
        for slot in slots:
            total = total + landing[pl.ds(slot * BLOCK + first, count), :].astype(F32)
        out[rows, :] = total.astype(BF16)

    def far_step(tree):
        term = group_term(tree, 3)
        tree[1][block(6), :] = term[:BLOCK]
        tree[2][block(7), :] = term[BLOCK:].astype(BF16)
        send(tree, "far_a", 7, 0, HALF, 0, 0, 1)
        send(tree, "far_b", 7, HALF, HALF, 0, 0, 1)

    def ring_step(tree):
        tree[2][rows_of(2), :] = group_term(tree, 2).astype(BF16)
        for part, name in ((0, "a"), (HALF, "b")):
            send(tree, "zup_" + name, 4, part, HALF, 1, 1, 0)
            send(tree, "zdown_" + name, 5, part, HALF, 2, 3, 0)

    def turn_step(tree):
        copies.arrived(tree[0] + "far_a")
        lower(tree, 6, 0, HALF, (0,))
        send(tree, "down2_g", 6, 0, HALF, 3, 3, 0)
        copies.arrived(tree[0] + "far_b")
        lower(tree, 6, HALF, HALF, (0,))
        send(tree, "up2_g", 6, HALF, HALF, 3, 1, 0)

    def free_step(tree):
        term = group_term(tree, 1)
        tree[2][half(2, 0), :] = term[:HALF].astype(BF16)
        tree[1][half(2, 1), :] = term[HALF : 2 * HALF]
        tree[1][half(3, 0), :] = term[2 * HALF : 3 * HALF]
        tree[2][half(3, 1), :] = term[3 * HALF :].astype(BF16)
        send(tree, "up_free", 2, 0, HALF, 4, 1, 0)
        send(tree, "down_free", 3, HALF, HALF, 5, 3, 0)

    def own_step(tree):
        tree[1][rows_of(0), :] = group_term(tree, 0)

    def pair_step(tree):
        for first, name in ((0, "a"), (HALF, "b")):
            copies.arrived(tree[0] + "zup_" + name)
            copies.arrived(tree[0] + "zdown_" + name)
            lower(tree, 1, first, HALF, (1, 2))
            send(tree, "z_" + name, 1, first, HALF, 6, 0, 1)

    def last_step(tree):
        copies.arrived(tree[0] + "up2_g")
        lower(tree, 2, HALF, HALF, (3,))
        send(tree, "up_last", 2, HALF, HALF, 4, 1, 0)
        copies.arrived(tree[0] + "down2_g")
        lower(tree, 3, 0, HALF, (3,))
        send(tree, "down_last", 3, 0, HALF, 5, 3, 0)

    image_tree, text_tree = trees
    weigh(6, 7)
    put_back(6, 7)
    far_step(image_tree)
    weigh(4, 5)
    put_back(4, 5)
    ring_step(image_tree)
    weigh(2, 3, 0, 1)
    put_back(2, 3, 0, 1)
    sums_a[0, 0:1, :] = own_lse - 2.0 * extra[0:1, :]
    sums_a[0, 1:2, :] = jnp.sum(heats[0] + heats[1] + heats[2] + heats[3], axis=0, keepdims=True) + extra[1:2, :]
    sums_a[0, 2:8, :] = jnp.zeros((6, 128), F32)
    for r, q in img_offsets:
        index = PLACE[(4 - r) % 4, q]
        copies.start("ai%d" % index, sums_a.at[0], sums_a.at[index], img_peer(r, q))

    core_step(3)
    core_step(2)
    far_step(text_tree)
    ring_step(text_tree)
    turn_step(image_tree)
    core_step(1)
    core_step(0)
    free_step(image_tree)
    turn_step(text_tree)
    free_step(text_tree)
    for index in range(1, 8):
        copies.arrived("ai%d" % index)
    total = sums_a[0]
    for index in range(1, 8):
        total = total + sums_a[index]
    sums_b[0] = total
    for r, q, c in txt_offsets:
        index = 8 * c + PLACE[(4 - r) % 4, q]
        copies.start("at%d" % index, sums_b.at[0], sums_b.at[index], txt_peer(r, q, c))
    own_step(image_tree)
    pair_step(image_tree)
    last_step(image_tree)
    own_step(text_tree)
    pair_step(text_tree)
    last_step(text_tree)
    for index in range(1, 16):
        copies.arrived("at%d" % index)
    total = sums_b[0]
    for index in range(1, 16):
        total = total + sums_b[index]
    loss_ref[0, 0] = jnp.sum(total[0:1, :]) * (LN2 / (2.0 * PAIRS))
    temp_ref[0, 0] = jnp.sum(total[1:2, :]) * (LN2 / PAIRS)
    stores = []
    results = ((image_tree, image_ref, grad_image_hbm), (text_tree, text_ref, grad_text_hbm))
    for tree, source, result in results:
        label, acc, out, landing, peer = tree
        for name in ("up_free", "down_free", "z_a", "z_b", "up_last", "down_last"):
            copies.arrived(label + name)

        def finalize(index, carry, source=source, acc=acc, landing=landing):
            part = pl.ds(pl.multiple_of(index * 16, 16), 16)
            grad = acc[part, :]
            for slot in (4, 5, 6):
                grad = grad + landing[pl.ds(pl.multiple_of(slot * BLOCK + index * 16, 16), 16), :].astype(F32)
            grad = grad * scale
            rows = source[part, :]
            inverse = inverse_of(rows)
            unit = rows * inverse
            source[part, :] = inverse * (grad - unit * jnp.sum(unit * grad, axis=1, keepdims=True))
            return carry

        lax.fori_loop(0, BLOCK // 16, finalize, 0)
        stores.append(pltpu.make_async_copy(source, result, local_sems.at[2 + len(stores)]))
        stores[-1].start()
    copies.finish()
    for store in stores:
        store.wait()


def on_device(image_feat, text_feat, logit_temp):
    logit_scale = jnp.exp(logit_temp).reshape(1, 1)
    smem = pl.BlockSpec(memory_space=pltpu.SMEM)
    anywhere = pl.BlockSpec(memory_space=pl.ANY)
    one = jax.ShapeDtypeStruct((1, 1), F32)
    shape = jax.ShapeDtypeStruct((BLOCK, WIDTH), F32)
    mean_loss, grad_image, grad_text, temp_grad = pl.pallas_call(
        kernel,
        out_shape=(one, shape, shape, one),
        in_specs=[smem, anywhere, anywhere],
        out_specs=(smem, anywhere, anywhere, smem),
        scratch_shapes=[
            pltpu.VMEM((BLOCK, WIDTH), F32),
            pltpu.VMEM((BLOCK, WIDTH), F32),
            pltpu.VMEM((1024, WIDTH), BF16),
            pltpu.VMEM((2048, WIDTH), BF16),
            pltpu.VMEM((1024, 2048), F32),
            pltpu.VMEM((1024, 2048), BF16),
            pltpu.VMEM((1024, 128), F32),
            pltpu.VMEM((1024, 128), F32),
            pltpu.VMEM((8, 2048), F32),
            pltpu.VMEM((8, 2048), F32),
            pltpu.VMEM((1024, 128), F32),
            pltpu.VMEM((1, 2048), F32),
            pltpu.VMEM((8, BLOCK, BLOCK), F32),
            pltpu.VMEM((8, 128), F32),
            pltpu.VMEM((8, 16, 128), F32),
            pltpu.VMEM((16, 32, 128), F32),
            pltpu.VMEM((8, 8, 128), F32),
            pltpu.VMEM((16, 8, 128), F32),
            pltpu.VMEM((1024, WIDTH), F32),
            pltpu.VMEM((1024, WIDTH), F32),
            pltpu.VMEM((1024, WIDTH), BF16),
            pltpu.VMEM((1024, WIDTH), BF16),
            pltpu.VMEM((1024, WIDTH), BF16),
            pltpu.VMEM((7 * BLOCK, WIDTH), BF16),
            pltpu.VMEM((7 * BLOCK, WIDTH), BF16),
            pltpu.VMEM((1024, WIDTH), BF16),
            pltpu.SemaphoreType.DMA((128,)),
            pltpu.SemaphoreType.DMA((128,)),
            pltpu.SemaphoreType.DMA((4,)),
        ],
        compiler_params=pltpu.CompilerParams(
            collective_id=0, has_side_effects=True, vmem_limit_bytes=60 * 2**20
        ),
        cost_estimate=pl.CostEstimate(flops=16106127360, bytes_accessed=2621440, transcendentals=8388608),
    )(logit_scale, image_feat, text_feat)
    return (mean_loss[0, 0], grad_image, grad_text, temp_grad[0, 0])


def solution(mesh):
    in_specs = (P(("img", "txt"), None), P(("txt", "img"), None), P())
    out_specs = (P(), P(("img", "txt"), None), P(("txt", "img"), None), P())
    return jax.shard_map(
        on_device, mesh=mesh, in_specs=in_specs, out_specs=out_specs, check_vma=False
    )
```

```python
import functools

import jax
import jax.numpy as jnp
from jax import lax
from jax.experimental import pallas as pl
from jax.experimental.pallas import tpu as pltpu
from jax.sharding import PartitionSpec as P

PLACE = {(0, 0): 0, (0, 1): 1, (1, 0): 2, (3, 0): 3, (1, 1): 4, (3, 1): 5, (2, 0): 6, (2, 1): 7}
BLOCK = 128
HALF = 64
QUARTER = 32
WIDTH = 1280
PAIRS = 16384
GROUP = 256
LOG2E = 1.4426950408889634
LN2 = 0.6931471805599453
HIGH_SHIFT = 33.0
LOW_SHIFT = 86.0
LOW_CAP = 20.0
HIGH_LEAST = 2.0**-62
F32 = jnp.float32
BF16 = jnp.bfloat16


def mod4(v):
    return lax.rem(v + 4, 4)


class Copies:
    def __init__(self, send_sems, recv_sems):
        self.send_sems, self.recv_sems = send_sems, recv_sems
        self.table = {}

    def start(self, name, src, dst, device):
        index = len(self.table)
        copy = pltpu.make_async_remote_copy(
            src_ref=src,
            dst_ref=dst,
            send_sem=self.send_sems.at[index],
            recv_sem=self.recv_sems.at[index],
            device_id=device,
            device_id_type=pl.DeviceIdType.MESH,
        )
        copy.start()
        self.table[name] = copy

    def arrived(self, name):
        self.table[name].wait_recv()

    def finish(self):
        for copy in self.table.values():
            copy.wait_send()


def kernel(
    scale_ref,
    image_hbm,
    text_hbm,
    totals_ref,
    sum_image_hbm,
    sum_text_hbm,
    image_ref,
    text_ref,
    img,
    txt,
    dots,
    wts,
    row1,
    row2,
    col1,
    col2,
    row_shift,
    col_shift,
    diagonals,
    extra,
    img_stats,
    txt_stats,
    sums_a,
    sums_b,
    img_acc,
    txt_acc,
    img_out,
    txt_out,
    core_out,
    img_in,
    txt_in,
    core_in,
    send_sems,
    recv_sems,
    local_sems,
):
    img_index = lax.axis_index("img")
    txt_index = lax.axis_index("txt")
    x, core = img_index // 2, lax.rem(img_index, 2)
    y, z = txt_index // 4, lax.rem(txt_index, 4)
    odd = lax.rem(z, 2)
    z_img = z + 1 - 2 * odd
    z_txt = mod4(z - 1 + 2 * odd)

    def img_peer(r, q):
        return (img_index, mod4(y + r) * 4 + (z_img if q else z))

    def txt_peer(r, q, c=0):
        return (
            mod4(x + r) * 2 + (1 - core if c else core),
            y * 4 + (z_txt if q else z),
        )

    img_offsets = [(r, q) for r in range(4) for q in range(2) if (r, q) != (0, 0)]
    txt_offsets = [
        (r, q, c) for r in range(4) for q in range(2) for c in range(2) if (r, q, c) != (0, 0, 0)
    ]
    load_image = pltpu.make_async_copy(image_hbm, image_ref, local_sems.at[0])
    load_text = pltpu.make_async_copy(text_hbm, text_ref, local_sems.at[1])
    load_image.start()
    load_text.start()
    barrier = pltpu.get_barrier_semaphore()
    for offset in img_offsets:
        pl.semaphore_signal(barrier, inc=1, device_id=img_peer(*offset), device_id_type=pl.DeviceIdType.MESH)
    for offset in txt_offsets:
        pl.semaphore_signal(barrier, inc=1, device_id=txt_peer(*offset), device_id_type=pl.DeviceIdType.MESH)

    scale = scale_ref[0, 0]
    slope = scale * LOG2E

    def inverse_of(rows):
        return lax.rsqrt(jnp.sum(rows * rows, axis=1, keepdims=True) + 1e-06)

    def normalize(source, target):
        def step(index, carry):
            part = pl.ds(pl.multiple_of(index * 16, 16), 16)
            rows = source[part, :]
            target[part, :] = (rows * inverse_of(rows)).astype(BF16)
            return carry

        lax.fori_loop(0, BLOCK // 16, step, 0)

    load_image.wait()
    normalize(image_ref, img)
    load_text.wait()
    normalize(text_ref, txt)
    pl.semaphore_wait(barrier, len(img_offsets) + len(txt_offsets))

    copies = Copies(send_sems, recv_sems)

    def half(place, part):
        return pl.ds(place * BLOCK + part * HALF, HALF)

    sides = (("i", img, img_peer), ("t", txt, txt_peer))

    def push(side, name, place, first, count, to_place, r, q):
        label, rows, peer = side
        copies.start(
            label + name + str(first),
            rows.at[pl.ds(place * BLOCK + first, count)],
            rows.at[pl.ds(to_place * BLOCK + first, count)],
            peer(r, q),
        )

    def to_core(place, first, count):
        copies.start(
            "c%d_%d" % (place, first),
            txt.at[pl.ds(place * BLOCK + first, count)],
            txt.at[pl.ds((8 + place) * BLOCK + first, count)],
            txt_peer(0, 0, 1),
        )

    for side in sides:
        push(side, "up", 0, 0, QUARTER, PLACE[3, 0], 1, 0)
        push(side, "down", 0, 64, QUARTER, PLACE[1, 0], 3, 0)
        push(side, "z", 0, 0, HALF, PLACE[0, 1], 0, 1)
    for side in sides:
        push(side, "up", 0, 32, QUARTER, PLACE[3, 0], 1, 0)
        push(side, "down", 0, 96, QUARTER, PLACE[1, 0], 3, 0)
        push(side, "up", 0, 64, HALF, PLACE[3, 0], 1, 0)
        push(side, "down", 0, 0, HALF, PLACE[1, 0], 3, 0)
        push(side, "z", 0, 64, HALF, PLACE[0, 1], 0, 1)
    to_core(0, 0, BLOCK)

    row1[...] = jnp.zeros_like(row1)
    row2[...] = jnp.zeros_like(row2)
    col1[...] = jnp.zeros_like(col1)
    col2[...] = jnp.zeros_like(col2)

    def forward(row, row_count, column, column_count):
        cols = pl.ds(column, column_count)
        product = lax.dot_general(
            img[pl.ds(row, row_count), :],
            txt[cols, :],
            (((1,), (1,)), ((), ())),
            preferred_element_type=F32,
        )
        dots[pl.ds(row, row_count), cols] = product * slope

        for first in range(row, row + row_count, 32):
            part = pl.ds(first, 32)
            add1 = jnp.zeros((32, 128), F32)
            add2 = jnp.zeros((32, 128), F32)
            for lane in range(column, column + column_count, 128):
                block_cols = pl.ds(lane, 128)
                score = dots[part, block_cols]
                mass1 = jnp.exp2(score - HIGH_SHIFT)
                mass2 = jnp.exp2(jnp.minimum(score, LOW_CAP) + LOW_SHIFT)
                add1 = add1 + mass1
                add2 = add2 + mass2
                col1[:, block_cols] += jnp.sum(mass1.reshape(32 // 8, 8, 128), axis=0)
                col2[:, block_cols] += jnp.sum(mass2.reshape(32 // 8, 8, 128), axis=0)
            row1[part, :] += add1
            row2[part, :] += add2

    def wait_core(*names):
        for name in names:
            copies.arrived("c" + name)

    def take(name, first):
        for side in sides:
            copies.arrived(side[0] + name + str(first))

    for first in (0, 32):
        for side in sides:
            copies.arrived(side[0] + "up" + str(first))
            push(side, "up2_", PLACE[3, 0], first, QUARTER, PLACE[2, 0], 1, 0)
            copies.arrived(side[0] + "down" + str(64 + first))
            push(side, "down2_", PLACE[1, 0], 64 + first, QUARTER, PLACE[2, 0], 3, 0)
    to_core(PLACE[3, 0], 0, HALF)
    to_core(PLACE[1, 0], 64, HALF)
    take("up", 64)
    take("down", 0)
    to_core(PLACE[3, 0], 64, HALF)
    to_core(PLACE[1, 0], 0, HALF)
    for first in (0, 64):
        for side in sides:
            copies.arrived(side[0] + "z" + str(first))
            push(side, "zup", PLACE[0, 1], first, HALF, PLACE[3, 1], 1, 0)
            push(side, "zdown", PLACE[0, 1], first, HALF, PLACE[1, 1], 3, 0)
    to_core(PLACE[0, 1], 0, BLOCK)
    for first in (0, 32):
        for side in sides:
            copies.arrived(side[0] + "up2_" + str(first))
            push(side, "up2z", PLACE[2, 0], first, QUARTER, PLACE[2, 1], 0, 1)
            copies.arrived(side[0] + "down2_" + str(64 + first))
            push(side, "down2z", PLACE[2, 0], 64 + first, QUARTER, PLACE[2, 1], 0, 1)
    to_core(PLACE[2, 0], 0, BLOCK)
    forward(0, 512, 0, 512)
    wait_core("0_0", "1_0", "2_0", "2_64", "3_0", "3_64", "6_0")
    forward(0, 512, 1024, 512)
    take("zup", 0)
    take("zdown", 0)
    to_core(PLACE[3, 1], 0, HALF)
    to_core(PLACE[1, 1], 0, HALF)
    forward(768, 128, 0, 512)
    forward(768, 128, 1024, 512)
    take("up2z", 0)
    take("down2z", 64)
    take("up2z", 32)
    take("down2z", 96)
    to_core(PLACE[2, 1], 0, BLOCK)
    take("zup", 64)
    take("zdown", 64)
    to_core(PLACE[3, 1], 64, HALF)
    to_core(PLACE[1, 1], 64, HALF)
    forward(512, 256, 0, 1024)
    forward(896, 128, 0, 512)
    wait_core("7_0", "4_0", "5_0", "4_64", "5_64")
    forward(0, 512, 512, 512)
    forward(768, 256, 512, 512)
    forward(512, 256, 1024, 1024)
    forward(896, 128, 1024, 512)
    forward(0, 512, 1536, 512)
    forward(768, 256, 1536, 512)

    def img_order(r, q):
        return mod4(y + r) * 2 + (1 - odd if q else odd)

    def txt_order(r, q, c):
        return (mod4(x + r) * 2 + (odd if q else 1 - odd)) * 2 + (1 - core if c else core)

    for (r, q), place in PLACE.items():
        rows = pl.ds(place * BLOCK, BLOCK)
        where = img_order(r, q)
        img_stats[0, pl.ds(where, 1), :] = jnp.sum(row1[rows, :].T, axis=0, keepdims=True)
        img_stats[0, pl.ds(8 + where, 1), :] = jnp.sum(row2[rows, :].T, axis=0, keepdims=True)
    for r, q in img_offsets:
        index = PLACE[(4 - r) % 4, q]
        copies.start("si%d" % index, img_stats.at[0], img_stats.at[index], img_peer(r, q))
    for (r, q), place in PLACE.items():
        for c in range(2):
            cols = pl.ds((8 * c + place) * BLOCK, BLOCK)
            where = txt_order(r, q, c)
            txt_stats[0, pl.ds(where, 1), :] = jnp.sum(col1[:, cols], axis=0, keepdims=True)
            txt_stats[0, pl.ds(16 + where, 1), :] = jnp.sum(col2[:, cols], axis=0, keepdims=True)
    for r, q, c in txt_offsets:
        index = 8 * c + PLACE[(4 - r) % 4, q]
        copies.start("st%d" % index, txt_stats.at[0], txt_stats.at[index], txt_peer(r, q, c))

    eye = lax.broadcasted_iota(jnp.int32, (BLOCK, BLOCK), 0) == lax.broadcasted_iota(jnp.int32, (BLOCK, BLOCK), 1)

    def on_diagonal(place, body):
        r, q = [key for key in PLACE if PLACE[key] == place][0]
        y_row, z_row = mod4(y + r), (z_img if q else z)
        x_text, z_text, core_text = lax.rem(y_row, 2) * 2 + z_row // 2, 2 * core + y_row // 2, lax.rem(z_row, 2)
        near = jnp.where(z_text == z, 1, 0)
        far = jnp.where(z_text == z_txt, 1, 0)
        ring = mod4(x_text - x)
        place_text = jnp.where(
            ring == 0, far, jnp.where(ring == 1, 2 + 2 * far, jnp.where(ring == 2, 6 + far, 3 + 2 * far))
        )
        place_text = place_text + 8 * jnp.where(core_text == core, 0, 1)

        @pl.when(jnp.where(x == y, near + far, 0) == 1)
        def _():
            body(pl.ds(place * BLOCK, BLOCK), pl.ds(pl.multiple_of(place_text * BLOCK, BLOCK), BLOCK))

    for place in range(8):

        def set_aside(rows, cols, place=place):
            scores = dots[rows, cols]
            diagonals[place] = scores
            dots[rows, cols] = jnp.where(eye, -10000.0, scores)

        on_diagonal(place, set_aside)

    def log_sum(high, low):
        return jnp.where(
            high >= HIGH_LEAST,
            jnp.log(high) * LOG2E + HIGH_SHIFT,
            jnp.log(jnp.maximum(low, 1e-37)) * LOG2E - LOW_SHIFT,
        )

    img_total = img_stats[0]
    for index in range(1, 8):
        copies.arrived("si%d" % index)
        img_total = img_total + img_stats[index]
    row_lse = log_sum(img_total[:8], img_total[8:])
    row1[0:8, :] = row_lse
    own_lse = row1[pl.ds(img_order(0, 0), 1), :]
    for (r, q), place in PLACE.items():
        one = row1[pl.ds(img_order(r, q), 1), :]
        row_shift[pl.ds(place * BLOCK, BLOCK), :] = jnp.broadcast_to(one + 1.0, (BLOCK, BLOCK)).T
    txt_total = txt_stats[0]
    for index in range(1, 16):
        copies.arrived("st%d" % index)
        txt_total = txt_total + txt_stats[index]
    col_lse = log_sum(txt_total[:16], txt_total[16:])
    row2[0:16, :] = col_lse
    own_lse = own_lse + row2[pl.ds(txt_order(0, 0, 0), 1), :]
    for (r, q), place in PLACE.items():
        for c in range(2):
            one = row2[pl.ds(txt_order(r, q, c), 1), :]
            col_shift[:, pl.ds((8 * c + place) * BLOCK, BLOCK)] = one + 1.0

    extra[...] = jnp.zeros_like(extra)
    heats = [jnp.zeros((16, 128), F32)] * 4

    def weigh(*places):
        for place in places:
            for first in range(place * BLOCK, place * BLOCK + BLOCK, 16):
                part = pl.ds(first, 16)
                shift = row_shift[part, :]
                for block in range(16):
                    cols = pl.ds(block * BLOCK, BLOCK)
                    score = dots[part, cols]
                    weight = jnp.exp2(score - shift) + jnp.exp2(score - col_shift[:, cols])
                    heats[block % 4] = heats[block % 4] + weight * score
                    wts[part, cols] = weight.astype(BF16)

    def put_back(*places):
        def body(place, rows, cols):
            scores = diagonals[place]
            weight = jnp.exp2(scores - row_shift[rows, :]) + jnp.exp2(scores - col_shift[:, cols])
            weight = jnp.where(eye, weight - 1.0, weight)
            wts[rows, cols] = weight.astype(BF16)
            extra[0:1, :] += jnp.sum(jnp.where(eye, scores, 0.0), axis=0, keepdims=True)
            extra[1:2, :] += jnp.sum(jnp.where(eye, weight * scores, 0.0), axis=0, keepdims=True)

        for place in places:
            on_diagonal(place, functools.partial(body, place))

    def block(place):
        return pl.ds(place * BLOCK, BLOCK)

    def rows_of(group):
        return pl.ds(group * GROUP, GROUP)

    def image_term(group):
        return jnp.dot(wts[rows_of(group), :], txt[...], preferred_element_type=F32)

    def text_term(group):
        return lax.dot_general(
            wts[:, rows_of(group)], img[...], (((0,), (0,)), ((), ())), preferred_element_type=F32
        )

    def core_step(group):
        rows = rows_of(group)
        core_out[rows, :] = text_term(4 + group).astype(BF16)
        copies.start("k%d" % group, core_out.at[rows], core_in.at[rows], txt_peer(0, 0, 1))

    def text_group(group):
        term = text_term(group)
        copies.arrived("k%d" % group)
        return term + core_in[rows_of(group), :].astype(F32)

    trees = (("i", img_acc, img_out, img_in, img_peer), ("t", txt_acc, txt_out, txt_in, txt_peer))

    def group_term(tree, group):
        return image_term(group) if tree[0] == "i" else text_group(group)

    def send(tree, name, place, first, count, to_place, r, q):
        label, acc, out, landing, peer = tree
        rows = pl.ds(place * BLOCK + first, count)
        copies.start(label + name, out.at[rows], landing.at[pl.ds(to_place * BLOCK + first, count)], peer(r, q))

    def lower(tree, place, first, count, slots):
        label, acc, out, landing, peer = tree
        rows = pl.ds(place * BLOCK + first, count)
        total = acc[rows, :]
        for slot in slots:
            total = total + landing[pl.ds(slot * BLOCK + first, count), :].astype(F32)
        out[rows, :] = total.astype(BF16)

    def ring_step(tree):
        tree[2][rows_of(2), :] = group_term(tree, 2).astype(BF16)
        for first in (0, HALF):
            send(tree, "zup_g%d" % first, 4, first, HALF, 1, 1, 0)
            send(tree, "zdown_g%d" % first, 5, first, HALF, 2, 3, 0)

    def far_step(tree):
        term = group_term(tree, 3)
        tree[1][block(6), :] = term[:BLOCK]
        tree[2][block(7), :] = term[BLOCK:].astype(BF16)
        for first in (0, 64, 32, 96):
            send(tree, "far_g%d" % first, 7, first, QUARTER, 0, 0, 1)

    def turn_step(tree, first):
        copies.arrived(tree[0] + "far_g%d" % first)
        lower(tree, 6, first, QUARTER, (0,))
        send(tree, "down2_g%d" % first, 6, first, QUARTER, 3, 3, 0)
        copies.arrived(tree[0] + "far_g%d" % (64 + first))
        lower(tree, 6, 64 + first, QUARTER, (0,))
        send(tree, "up2_g%d" % first, 6, 64 + first, QUARTER, 3, 1, 0)

    def free_step(tree):
        term = group_term(tree, 1)
        tree[2][half(2, 0), :] = term[:HALF].astype(BF16)
        tree[1][half(2, 1), :] = term[HALF : 2 * HALF]
        tree[1][half(3, 0), :] = term[2 * HALF : 3 * HALF]
        tree[2][half(3, 1), :] = term[3 * HALF :].astype(BF16)
        send(tree, "up_free", 2, 0, HALF, 4, 1, 0)
        send(tree, "down_free", 3, HALF, HALF, 5, 3, 0)

    def own_step(tree):
        tree[1][rows_of(0), :] = group_term(tree, 0)

    def pair_step(tree, first):
        copies.arrived(tree[0] + "zup_g%d" % first)
        copies.arrived(tree[0] + "zdown_g%d" % first)
        lower(tree, 1, first, HALF, (1, 2))
        send(tree, "z_g%d" % first, 1, first, HALF, 6, 0, 1)

    def last_step(tree, first):
        copies.arrived(tree[0] + "up2_g%d" % first)
        lower(tree, 2, 64 + first, QUARTER, (3,))
        send(tree, "up_last%d" % first, 2, 64 + first, QUARTER, 4, 1, 0)
        copies.arrived(tree[0] + "down2_g%d" % first)
        lower(tree, 3, first, QUARTER, (3,))
        send(tree, "down_last%d" % first, 3, first, QUARTER, 5, 3, 0)

    image_tree, text_tree = trees
    weigh(*range(8))
    put_back(*range(8))
    core_step(2)
    ring_step(image_tree)
    sums_a[0, 0:1, :] = own_lse - 2.0 * extra[0:1, :]
    sums_a[0, 1:2, :] = jnp.sum(heats[0] + heats[1] + heats[2] + heats[3], axis=0, keepdims=True) + extra[1:2, :]
    sums_a[0, 2:8, :] = jnp.zeros((6, 128), F32)
    for r, q in img_offsets:
        index = PLACE[(4 - r) % 4, q]
        copies.start("ai%d" % index, sums_a.at[0], sums_a.at[index], img_peer(r, q))

    ring_step(text_tree)
    core_step(3)
    far_step(image_tree)
    far_step(text_tree)
    core_step(1)
    core_step(0)
    free_step(image_tree)
    free_step(text_tree)
    for index in range(1, 8):
        copies.arrived("ai%d" % index)
    total = sums_a[0]
    for index in range(1, 8):
        total = total + sums_a[index]
    sums_b[0] = total
    for r, q, c in txt_offsets:
        index = 8 * c + PLACE[(4 - r) % 4, q]
        copies.start("at%d" % index, sums_b.at[0], sums_b.at[index], txt_peer(r, q, c))
    own_step(image_tree)
    own_step(text_tree)
    turn_step(image_tree, 0)
    turn_step(text_tree, 0)
    for tree in trees:
        pair_step(tree, 0)
        pair_step(tree, HALF)
    turn_step(image_tree, QUARTER)
    turn_step(text_tree, QUARTER)
    for first in (0, QUARTER):
        for tree in trees:
            last_step(tree, first)
    for index in range(1, 16):
        copies.arrived("at%d" % index)
    total = sums_b[0]
    for index in range(1, 16):
        total = total + sums_b[index]
    totals_ref[...] = total
    stores = []
    for tree, source, result in ((image_tree, image_ref, sum_image_hbm), (text_tree, text_ref, sum_text_hbm)):
        label, acc, out, landing, peer = tree
        for name in ("up_free", "down_free", "z_g0", "z_g64", "up_last0", "down_last0", "up_last32", "down_last32"):
            copies.arrived(label + name)
        grad = acc[block(0), :]
        for slot in (4, 5, 6):
            grad = grad + landing[block(slot), :].astype(F32)
        source[...] = grad
        stores.append(pltpu.make_async_copy(source, result, local_sems.at[2 + len(stores)]))
        stores[-1].start()
    copies.finish()
    for store in stores:
        store.wait()


def finalize(scale_ref, totals_ref, image_ref, text_ref, sum_image_ref, sum_text_ref, loss_ref, grad_image_ref, grad_text_ref, temp_ref):
    scale = scale_ref[0, 0]
    for source, total, result in (
        (image_ref, sum_image_ref, grad_image_ref),
        (text_ref, sum_text_ref, grad_text_ref),
    ):
        rows = source[...]
        inverse = lax.rsqrt(jnp.sum(rows * rows, axis=1, keepdims=True) + 1e-06)
        grad = total[...] * scale
        unit = rows * inverse
        result[...] = inverse * (grad - unit * jnp.sum(unit * grad, axis=1, keepdims=True))
    totals = totals_ref[...]
    loss_ref[0, 0] = jnp.sum(totals[0:1, :]) * (LN2 / (2.0 * PAIRS))
    temp_ref[0, 0] = jnp.sum(totals[1:2, :]) * (LN2 / PAIRS)


def on_device(image_feat, text_feat, logit_temp):
    logit_scale = jnp.exp(logit_temp).reshape(1, 1)
    smem = pl.BlockSpec(memory_space=pltpu.SMEM)
    anywhere = pl.BlockSpec(memory_space=pl.ANY)
    one = jax.ShapeDtypeStruct((1, 1), F32)
    shape = jax.ShapeDtypeStruct((BLOCK, WIDTH), F32)
    totals, sum_image, sum_text = pl.pallas_call(
        kernel,
        out_shape=(jax.ShapeDtypeStruct((8, 128), F32), shape, shape),
        in_specs=[smem, anywhere, anywhere],
        out_specs=(pl.BlockSpec(memory_space=pltpu.VMEM), anywhere, anywhere),
        scratch_shapes=[
            pltpu.VMEM((BLOCK, WIDTH), F32),
            pltpu.VMEM((BLOCK, WIDTH), F32),
            pltpu.VMEM((1024, WIDTH), BF16),
            pltpu.VMEM((2048, WIDTH), BF16),
            pltpu.VMEM((1024, 2048), F32),
            pltpu.VMEM((1024, 2048), BF16),
            pltpu.VMEM((1024, 128), F32),
            pltpu.VMEM((1024, 128), F32),
            pltpu.VMEM((8, 2048), F32),
            pltpu.VMEM((8, 2048), F32),
            pltpu.VMEM((1024, 128), F32),
            pltpu.VMEM((1, 2048), F32),
            pltpu.VMEM((8, BLOCK, BLOCK), F32),
            pltpu.VMEM((8, 128), F32),
            pltpu.VMEM((8, 16, 128), F32),
            pltpu.VMEM((16, 32, 128), F32),
            pltpu.VMEM((8, 8, 128), F32),
            pltpu.VMEM((16, 8, 128), F32),
            pltpu.VMEM((1024, WIDTH), F32),
            pltpu.VMEM((1024, WIDTH), F32),
            pltpu.VMEM((1024, WIDTH), BF16),
            pltpu.VMEM((1024, WIDTH), BF16),
            pltpu.VMEM((1024, WIDTH), BF16),
            pltpu.VMEM((7 * BLOCK, WIDTH), BF16),
            pltpu.VMEM((7 * BLOCK, WIDTH), BF16),
            pltpu.VMEM((1024, WIDTH), BF16),
            pltpu.SemaphoreType.DMA((160,)),
            pltpu.SemaphoreType.DMA((160,)),
            pltpu.SemaphoreType.DMA((4,)),
        ],
        compiler_params=pltpu.CompilerParams(
            collective_id=0, has_side_effects=True, vmem_limit_bytes=60 * 2**20
        ),
        cost_estimate=pl.CostEstimate(flops=16106127360, bytes_accessed=2621440, transcendentals=8388608),
    )(logit_scale, image_feat, text_feat)
    step_rows = 32
    rows = pl.BlockSpec((step_rows, WIDTH), lambda i: (i, 0))
    mean_loss, grad_image, grad_text, temp_grad = pl.pallas_call(
        finalize,
        grid=(BLOCK // step_rows,),
        out_shape=(one, shape, shape, one),
        in_specs=[smem, pl.BlockSpec((8, 128), lambda i: (0, 0)), rows, rows, rows, rows],
        out_specs=(smem, rows, rows, smem),
    )(logit_scale, totals, image_feat, text_feat, sum_image, sum_text)
    return (mean_loss[0, 0], grad_image, grad_text, temp_grad[0, 0])


def solution(mesh):
    in_specs = (P(("img", "txt"), None), P(("txt", "img"), None), P())
    out_specs = (P(), P(("img", "txt"), None), P(("txt", "img"), None), P())
    return jax.shard_map(
        on_device, mesh=mesh, in_specs=in_specs, out_specs=out_specs, check_vma=False
    )
```

```python
import functools

import jax
import jax.numpy as jnp
from jax import lax
from jax.experimental import pallas as pl
from jax.experimental.pallas import tpu as pltpu
from jax.sharding import PartitionSpec as P

PLACE = {(0, 0): 0, (0, 1): 1, (1, 0): 2, (3, 0): 3, (1, 1): 4, (3, 1): 5, (2, 0): 6, (2, 1): 7}
BLOCK = 128
HALF = 64
QUARTER = 32
WIDTH = 1280
PAIRS = 16384
GROUP = 256
LOG2E = 1.4426950408889634
LN2 = 0.6931471805599453
HIGH_SHIFT = 33.0
LOW_SHIFT = 86.0
LOW_CAP = 20.0
HIGH_LEAST = 2.0**-62
F32 = jnp.float32
BF16 = jnp.bfloat16


def exp_of(temp):
    return jnp.max(jnp.exp(jnp.full((8, 128), temp, F32)))


def mod4(v):
    return lax.rem(v + 4, 4)


class Copies:
    def __init__(self, send_sems, recv_sems):
        self.send_sems, self.recv_sems = send_sems, recv_sems
        self.table = {}

    def start(self, name, src, dst, device):
        index = len(self.table)
        copy = pltpu.make_async_remote_copy(
            src_ref=src,
            dst_ref=dst,
            send_sem=self.send_sems.at[index],
            recv_sem=self.recv_sems.at[index],
            device_id=device,
            device_id_type=pl.DeviceIdType.MESH,
        )
        copy.start()
        self.table[name] = copy

    def arrived(self, name):
        self.table[name].wait_recv()

    def finish(self):
        for copy in self.table.values():
            copy.wait_send()


def kernel(
    temp_ref,
    image_hbm,
    text_hbm,
    totals_ref,
    sum_image_hbm,
    sum_text_hbm,
    image_ref,
    text_ref,
    img,
    txt,
    dots,
    wts,
    row1,
    row2,
    col1,
    col2,
    row_shift,
    col_shift,
    diagonals,
    extra,
    img_stats,
    txt_stats,
    sums_a,
    sums_b,
    img_acc,
    txt_acc,
    img_out,
    txt_out,
    core_out,
    img_in,
    txt_in,
    core_in,
    send_sems,
    recv_sems,
    local_sems,
):
    img_index = lax.axis_index("img")
    txt_index = lax.axis_index("txt")
    x, core = img_index // 2, lax.rem(img_index, 2)
    y, z = txt_index // 4, lax.rem(txt_index, 4)
    odd = lax.rem(z, 2)
    z_img = z + 1 - 2 * odd
    z_txt = mod4(z - 1 + 2 * odd)

    def img_peer(r, q):
        return (img_index, mod4(y + r) * 4 + (z_img if q else z))

    def txt_peer(r, q, c=0):
        return (
            mod4(x + r) * 2 + (1 - core if c else core),
            y * 4 + (z_txt if q else z),
        )

    img_offsets = [(r, q) for r in range(4) for q in range(2) if (r, q) != (0, 0)]
    txt_offsets = [
        (r, q, c) for r in range(4) for q in range(2) for c in range(2) if (r, q, c) != (0, 0, 0)
    ]
    load_image = pltpu.make_async_copy(image_hbm, image_ref, local_sems.at[0])
    load_text = pltpu.make_async_copy(text_hbm, text_ref, local_sems.at[1])
    load_image.start()
    load_text.start()
    barrier = pltpu.get_barrier_semaphore()
    for offset in img_offsets:
        pl.semaphore_signal(barrier, inc=1, device_id=img_peer(*offset), device_id_type=pl.DeviceIdType.MESH)
    for offset in txt_offsets:
        pl.semaphore_signal(barrier, inc=1, device_id=txt_peer(*offset), device_id_type=pl.DeviceIdType.MESH)

    scale = exp_of(temp_ref[0, 0])
    slope = scale * LOG2E

    def inverse_of(rows):
        return lax.rsqrt(jnp.sum(rows * rows, axis=1, keepdims=True) + 1e-06)

    def normalize(source, target):
        for first in range(0, BLOCK, 32):
            rows = source[first : first + 32, :]
            target[first : first + 32, :] = (rows * inverse_of(rows)).astype(BF16)

    load_image.wait()
    normalize(image_ref, img)
    pl.semaphore_wait(barrier, len(img_offsets) + len(txt_offsets))

    copies = Copies(send_sems, recv_sems)

    def half(place, part):
        return pl.ds(place * BLOCK + part * HALF, HALF)

    sides = (("i", img, img_peer), ("t", txt, txt_peer))

    def push(side, name, place, first, count, to_place, r, q):
        label, rows, peer = side
        copies.start(
            label + name + str(first),
            rows.at[pl.ds(place * BLOCK + first, count)],
            rows.at[pl.ds(to_place * BLOCK + first, count)],
            peer(r, q),
        )

    def to_core(place, first, count):
        copies.start(
            "c%d_%d" % (place, first),
            txt.at[pl.ds(place * BLOCK + first, count)],
            txt.at[pl.ds((8 + place) * BLOCK + first, count)],
            txt_peer(0, 0, 1),
        )

    def push_own(side):
        push(side, "up", 0, 0, QUARTER, PLACE[3, 0], 1, 0)
        push(side, "down", 0, 64, QUARTER, PLACE[1, 0], 3, 0)
        push(side, "z", 0, 0, HALF, PLACE[0, 1], 0, 1)
        push(side, "up", 0, 32, QUARTER, PLACE[3, 0], 1, 0)
        push(side, "down", 0, 96, QUARTER, PLACE[1, 0], 3, 0)
        push(side, "up", 0, 64, HALF, PLACE[3, 0], 1, 0)
        push(side, "down", 0, 0, HALF, PLACE[1, 0], 3, 0)
        push(side, "z", 0, 64, HALF, PLACE[0, 1], 0, 1)

    push_own(sides[0])
    load_text.wait()
    normalize(text_ref, txt)
    push_own(sides[1])
    to_core(0, 0, BLOCK)

    row1[...] = jnp.zeros_like(row1)
    row2[...] = jnp.zeros_like(row2)
    col1[...] = jnp.zeros_like(col1)
    col2[...] = jnp.zeros_like(col2)

    def forward(row, row_count, column, column_count):
        cols = pl.ds(column, column_count)
        product = lax.dot_general(
            img[pl.ds(row, row_count), :],
            txt[cols, :],
            (((1,), (1,)), ((), ())),
            preferred_element_type=F32,
        )
        dots[pl.ds(row, row_count), cols] = product * slope

        for first in range(row, row + row_count, 32):
            part = pl.ds(first, 32)
            add1 = jnp.zeros((32, 128), F32)
            add2 = jnp.zeros((32, 128), F32)
            for lane in range(column, column + column_count, 128):
                block_cols = pl.ds(lane, 128)
                score = dots[part, block_cols]
                mass1 = jnp.exp2(score - HIGH_SHIFT)
                mass2 = jnp.exp2(jnp.minimum(score, LOW_CAP) + LOW_SHIFT)
                add1 = add1 + mass1
                add2 = add2 + mass2
                col1[:, block_cols] += jnp.sum(mass1.reshape(32 // 8, 8, 128), axis=0)
                col2[:, block_cols] += jnp.sum(mass2.reshape(32 // 8, 8, 128), axis=0)
            row1[part, :] += add1
            row2[part, :] += add2

    def wait_core(*names):
        for name in names:
            copies.arrived("c" + name)

    def take(name, first):
        for side in sides:
            copies.arrived(side[0] + name + str(first))

    for first in (0, 32):
        for side in sides:
            copies.arrived(side[0] + "up" + str(first))
            push(side, "up2_", PLACE[3, 0], first, QUARTER, PLACE[2, 0], 1, 0)
            copies.arrived(side[0] + "down" + str(64 + first))
            push(side, "down2_", PLACE[1, 0], 64 + first, QUARTER, PLACE[2, 0], 3, 0)
    to_core(PLACE[3, 0], 0, HALF)
    to_core(PLACE[1, 0], 64, HALF)
    take("up", 64)
    take("down", 0)
    to_core(PLACE[3, 0], 64, HALF)
    to_core(PLACE[1, 0], 0, HALF)
    for first in (0, 64):
        for side in sides:
            copies.arrived(side[0] + "z" + str(first))
            push(side, "zup", PLACE[0, 1], first, HALF, PLACE[3, 1], 1, 0)
            push(side, "zdown", PLACE[0, 1], first, HALF, PLACE[1, 1], 3, 0)
    to_core(PLACE[0, 1], 0, BLOCK)
    for first in (0, 32):
        for side in sides:
            copies.arrived(side[0] + "up2_" + str(first))
            push(side, "up2z", PLACE[2, 0], first, QUARTER, PLACE[2, 1], 0, 1)
            copies.arrived(side[0] + "down2_" + str(64 + first))
            push(side, "down2z", PLACE[2, 0], 64 + first, QUARTER, PLACE[2, 1], 0, 1)
    to_core(PLACE[2, 0], 0, BLOCK)
    forward(0, 512, 0, 512)
    wait_core("0_0", "1_0", "2_0", "2_64", "3_0", "3_64", "6_0")
    forward(0, 512, 1024, 512)
    take("zup", 0)
    take("zdown", 0)
    to_core(PLACE[3, 1], 0, HALF)
    to_core(PLACE[1, 1], 0, HALF)
    forward(768, 128, 0, 512)
    forward(768, 128, 1024, 512)
    take("up2z", 0)
    take("down2z", 64)
    take("up2z", 32)
    take("down2z", 96)
    to_core(PLACE[2, 1], 0, BLOCK)
    take("zup", 64)
    take("zdown", 64)
    to_core(PLACE[3, 1], 64, HALF)
    to_core(PLACE[1, 1], 64, HALF)
    forward(512, 256, 0, 1024)
    forward(896, 128, 0, 512)
    wait_core("7_0", "4_0", "5_0", "4_64", "5_64")
    forward(0, 512, 512, 512)
    forward(768, 256, 512, 512)
    forward(512, 256, 1024, 1024)
    forward(896, 128, 1024, 512)
    forward(0, 512, 1536, 512)
    forward(768, 256, 1536, 512)

    def img_order(r, q):
        return mod4(y + r) * 2 + (1 - odd if q else odd)

    def txt_order(r, q, c):
        return (mod4(x + r) * 2 + (odd if q else 1 - odd)) * 2 + (1 - core if c else core)

    for (r, q), place in PLACE.items():
        for c in range(2):
            cols = pl.ds((8 * c + place) * BLOCK, BLOCK)
            where = txt_order(r, q, c)
            txt_stats[0, pl.ds(where, 1), :] = jnp.sum(col1[:, cols], axis=0, keepdims=True)
            txt_stats[0, pl.ds(16 + where, 1), :] = jnp.sum(col2[:, cols], axis=0, keepdims=True)
    for r, q, c in txt_offsets:
        index = 8 * c + PLACE[(4 - r) % 4, q]
        copies.start("st%d" % index, txt_stats.at[0], txt_stats.at[index], txt_peer(r, q, c))
    for (r, q), place in PLACE.items():
        rows = pl.ds(place * BLOCK, BLOCK)
        where = img_order(r, q)
        img_stats[0, pl.ds(where, 1), :] = jnp.sum(row1[rows, :].T, axis=0, keepdims=True)
        img_stats[0, pl.ds(8 + where, 1), :] = jnp.sum(row2[rows, :].T, axis=0, keepdims=True)
    for r, q in img_offsets:
        index = PLACE[(4 - r) % 4, q]
        copies.start("si%d" % index, img_stats.at[0], img_stats.at[index], img_peer(r, q))

    eye = lax.broadcasted_iota(jnp.int32, (BLOCK, BLOCK), 0) == lax.broadcasted_iota(jnp.int32, (BLOCK, BLOCK), 1)

    def on_diagonal(place, body, wanted=lambda group: 1):
        r, q = [key for key in PLACE if PLACE[key] == place][0]
        y_row, z_row = mod4(y + r), (z_img if q else z)
        x_text, z_text, core_text = lax.rem(y_row, 2) * 2 + z_row // 2, 2 * core + y_row // 2, lax.rem(z_row, 2)
        near = jnp.where(z_text == z, 1, 0)
        far = jnp.where(z_text == z_txt, 1, 0)
        ring = mod4(x_text - x)
        place_text = jnp.where(
            ring == 0, far, jnp.where(ring == 1, 2 + 2 * far, jnp.where(ring == 2, 6 + far, 3 + 2 * far))
        )
        place_text = place_text + 8 * jnp.where(core_text == core, 0, 1)

        @pl.when(jnp.where(x == y, near + far, 0) * wanted(place_text // 2) == 1)
        def _():
            body(pl.ds(place * BLOCK, BLOCK), pl.ds(pl.multiple_of(place_text * BLOCK, BLOCK), BLOCK))

    for place in range(8):

        def set_aside(rows, cols, place=place):
            scores = dots[rows, cols]
            diagonals[place] = scores
            dots[rows, cols] = jnp.where(eye, -10000.0, scores)

        on_diagonal(place, set_aside)

    def log_sum(high, low):
        return jnp.where(
            high >= HIGH_LEAST,
            jnp.log(high) * LOG2E + HIGH_SHIFT,
            jnp.log(jnp.maximum(low, 1e-37)) * LOG2E - LOW_SHIFT,
        )

    img_total = img_stats[0]
    for index in range(1, 8):
        copies.arrived("si%d" % index)
        img_total = img_total + img_stats[index]
    row_lse = log_sum(img_total[:8], img_total[8:])
    row1[0:8, :] = row_lse
    own_lse = row1[pl.ds(img_order(0, 0), 1), :]
    for (r, q), place in PLACE.items():
        one = row1[pl.ds(img_order(r, q), 1), :]
        row_shift[pl.ds(place * BLOCK, BLOCK), :] = jnp.broadcast_to(one + 1.0, (BLOCK, BLOCK)).T
    txt_total = txt_stats[0]
    for index in range(1, 16):
        copies.arrived("st%d" % index)
        txt_total = txt_total + txt_stats[index]
    col_lse = log_sum(txt_total[:16], txt_total[16:])
    row2[0:16, :] = col_lse
    own_lse = own_lse + row2[pl.ds(txt_order(0, 0, 0), 1), :]
    for (r, q), place in PLACE.items():
        for c in range(2):
            one = row2[pl.ds(txt_order(r, q, c), 1), :]
            col_shift[:, pl.ds((8 * c + place) * BLOCK, BLOCK)] = one + 1.0

    extra[...] = jnp.zeros_like(extra)
    heats = [jnp.zeros((16, 128), F32)] * 4

    def weigh(places, blocks):
        for place in places:
            for first in range(place * BLOCK, place * BLOCK + BLOCK, 16):
                part = pl.ds(first, 16)
                shift = row_shift[part, :]
                for block in blocks:
                    cols = pl.ds(block * BLOCK, BLOCK)
                    score = dots[part, cols]
                    weight = jnp.exp2(score - shift) + jnp.exp2(score - col_shift[:, cols])
                    heats[block % 4] = heats[block % 4] + weight * score
                    wts[part, cols] = weight.astype(BF16)

    def put_back(places, wanted):
        def body(place, rows, cols):
            scores = diagonals[place]
            weight = jnp.exp2(scores - row_shift[rows, :]) + jnp.exp2(scores - col_shift[:, cols])
            weight = jnp.where(eye, weight - 1.0, weight)
            wts[rows, cols] = weight.astype(BF16)
            extra[0:1, :] += jnp.sum(jnp.where(eye, scores, 0.0), axis=0, keepdims=True)
            extra[1:2, :] += jnp.sum(jnp.where(eye, weight * scores, 0.0), axis=0, keepdims=True)

        for place in places:
            on_diagonal(place, functools.partial(body, place), wanted)

    def block(place):
        return pl.ds(place * BLOCK, BLOCK)

    def rows_of(group):
        return pl.ds(group * GROUP, GROUP)

    def image_term(group):
        return jnp.dot(wts[rows_of(group), :], txt[...], preferred_element_type=F32)

    def text_term(group):
        return lax.dot_general(
            wts[:, rows_of(group)], img[...], (((0,), (0,)), ((), ())), preferred_element_type=F32
        )

    def core_step(group):
        rows = rows_of(group)
        core_out[rows, :] = text_term(4 + group).astype(BF16)
        copies.start("k%d" % group, core_out.at[rows], core_in.at[rows], txt_peer(0, 0, 1))

    def text_group(group):
        term = text_term(group)
        copies.arrived("k%d" % group)
        return term + core_in[rows_of(group), :].astype(F32)

    trees = (("i", img_acc, img_out, img_in, img_peer), ("t", txt_acc, txt_out, txt_in, txt_peer))

    def group_term(tree, group):
        return image_term(group) if tree[0] == "i" else text_group(group)

    def send(tree, name, place, first, count, to_place, r, q):
        label, acc, out, landing, peer = tree
        rows = pl.ds(place * BLOCK + first, count)
        copies.start(label + name, out.at[rows], landing.at[pl.ds(to_place * BLOCK + first, count)], peer(r, q))

    def lower(tree, place, first, count, slots):
        label, acc, out, landing, peer = tree
        rows = pl.ds(place * BLOCK + first, count)
        total = acc[rows, :]
        for slot in slots:
            total = total + landing[pl.ds(slot * BLOCK + first, count), :].astype(F32)
        out[rows, :] = total.astype(BF16)

    def ring_step(tree):
        tree[2][rows_of(2), :] = group_term(tree, 2).astype(BF16)
        for first in (0, HALF):
            send(tree, "zup_g%d" % first, 4, first, HALF, 1, 1, 0)
            send(tree, "zdown_g%d" % first, 5, first, HALF, 2, 3, 0)

    def far_step(tree):
        term = group_term(tree, 3)
        tree[1][block(6), :] = term[:BLOCK]
        tree[2][block(7), :] = term[BLOCK:].astype(BF16)
        for first in (0, 64, 32, 96):
            send(tree, "far_g%d" % first, 7, first, QUARTER, 0, 0, 1)

    def turn_step(tree, first):
        copies.arrived(tree[0] + "far_g%d" % first)
        lower(tree, 6, first, QUARTER, (0,))
        send(tree, "down2_g%d" % first, 6, first, QUARTER, 3, 3, 0)
        copies.arrived(tree[0] + "far_g%d" % (64 + first))
        lower(tree, 6, 64 + first, QUARTER, (0,))
        send(tree, "up2_g%d" % first, 6, 64 + first, QUARTER, 3, 1, 0)

    def free_step(tree):
        term = group_term(tree, 1)
        tree[2][half(2, 0), :] = term[:HALF].astype(BF16)
        tree[1][half(2, 1), :] = term[HALF : 2 * HALF]
        tree[1][half(3, 0), :] = term[2 * HALF : 3 * HALF]
        tree[2][half(3, 1), :] = term[3 * HALF :].astype(BF16)
        send(tree, "up_free", 2, 0, HALF, 4, 1, 0)
        send(tree, "down_free", 3, HALF, HALF, 5, 3, 0)

    def own_step(tree):
        tree[1][rows_of(0), :] = group_term(tree, 0)

    def pair_step(tree, first):
        copies.arrived(tree[0] + "zup_g%d" % first)
        copies.arrived(tree[0] + "zdown_g%d" % first)
        lower(tree, 1, first, HALF, (1, 2))
        send(tree, "z_g%d" % first, 1, first, HALF, 6, 0, 1)

    def last_step(tree, first):
        copies.arrived(tree[0] + "up2_g%d" % first)
        lower(tree, 2, 64 + first, QUARTER, (3,))
        send(tree, "up_last%d" % first, 2, 64 + first, QUARTER, 4, 1, 0)
        copies.arrived(tree[0] + "down2_g%d" % first)
        lower(tree, 3, first, QUARTER, (3,))
        send(tree, "down_last%d" % first, 3, first, QUARTER, 5, 3, 0)

    image_tree, text_tree = trees
    weigh(range(8), range(16))
    put_back(range(8), lambda group: 1)
    sums_a[0, 0:1, :] = own_lse - 2.0 * extra[0:1, :]
    sums_a[0, 1:2, :] = jnp.sum(heats[0] + heats[1] + heats[2] + heats[3], axis=0, keepdims=True) + extra[1:2, :]
    sums_a[0, 2:8, :] = jnp.zeros((6, 128), F32)
    for r, q in img_offsets:
        index = PLACE[(4 - r) % 4, q]
        copies.start("ai%d" % index, sums_a.at[0], sums_a.at[index], img_peer(r, q))

    core_step(2)
    ring_step(image_tree)
    ring_step(text_tree)
    core_step(3)
    far_step(image_tree)
    far_step(text_tree)
    core_step(1)
    free_step(image_tree)
    free_step(text_tree)
    for index in range(1, 8):
        copies.arrived("ai%d" % index)
    total = sums_a[0]
    for index in range(1, 8):
        total = total + sums_a[index]
    sums_b[0] = total
    for r, q, c in txt_offsets:
        index = 8 * c + PLACE[(4 - r) % 4, q]
        copies.start("at%d" % index, sums_b.at[0], sums_b.at[index], txt_peer(r, q, c))
    core_step(0)
    own_step(image_tree)
    turn_step(image_tree, 0)
    own_step(text_tree)
    turn_step(text_tree, 0)
    pair_step(image_tree, 0)
    pair_step(image_tree, HALF)
    turn_step(image_tree, QUARTER)
    pair_step(text_tree, 0)
    pair_step(text_tree, HALF)
    turn_step(text_tree, QUARTER)
    for first in (0, QUARTER):
        for tree in trees:
            last_step(tree, first)
    for index in range(1, 16):
        copies.arrived("at%d" % index)
    total = sums_b[0]
    for index in range(1, 16):
        total = total + sums_b[index]
    totals_ref[...] = total
    stores = []
    for tree, source, result in ((image_tree, image_ref, sum_image_hbm), (text_tree, text_ref, sum_text_hbm)):
        label, acc, out, landing, peer = tree
        for name in ("up_free", "down_free", "z_g0", "z_g64", "up_last0", "down_last0", "up_last32", "down_last32"):
            copies.arrived(label + name)
        grad = acc[block(0), :]
        for slot in (4, 5, 6):
            grad = grad + landing[block(slot), :].astype(F32)
        source[...] = grad
        stores.append(pltpu.make_async_copy(source, result, local_sems.at[2 + len(stores)]))
        stores[-1].start()
    copies.finish()
    for store in stores:
        store.wait()


def finalize(
    temp_ref,
    totals_ref,
    image_ref,
    text_ref,
    sum_image_ref,
    sum_text_ref,
    loss_ref,
    grad_image_ref,
    grad_text_ref,
    temp_grad_ref,
):
    scale = exp_of(temp_ref[0, 0])
    for source, total, result in (
        (image_ref, sum_image_ref, grad_image_ref),
        (text_ref, sum_text_ref, grad_text_ref),
    ):
        rows = source[...]
        inverse = lax.rsqrt(jnp.sum(rows * rows, axis=1, keepdims=True) + 1e-06)
        grad = total[...] * scale
        unit = rows * inverse
        result[...] = inverse * (grad - unit * jnp.sum(unit * grad, axis=1, keepdims=True))
    totals = totals_ref[...]
    loss_ref[0, 0] = jnp.sum(totals[0:1, :]) * (LN2 / (2.0 * PAIRS))
    temp_grad_ref[0, 0] = jnp.sum(totals[1:2, :]) * (LN2 / PAIRS)


def on_device(image_feat, text_feat, logit_temp):
    logit_temp = logit_temp.reshape(1, 1)
    smem = pl.BlockSpec(memory_space=pltpu.SMEM)
    anywhere = pl.BlockSpec(memory_space=pl.ANY)
    one = jax.ShapeDtypeStruct((1, 1), F32)
    shape = jax.ShapeDtypeStruct((BLOCK, WIDTH), F32)
    totals, sum_image, sum_text = pl.pallas_call(
        kernel,
        out_shape=(jax.ShapeDtypeStruct((8, 128), F32), shape, shape),
        in_specs=[smem, anywhere, anywhere],
        out_specs=(pl.BlockSpec(memory_space=pltpu.VMEM), anywhere, anywhere),
        scratch_shapes=[
            pltpu.VMEM((BLOCK, WIDTH), F32),
            pltpu.VMEM((BLOCK, WIDTH), F32),
            pltpu.VMEM((1024, WIDTH), BF16),
            pltpu.VMEM((2048, WIDTH), BF16),
            pltpu.VMEM((1024, 2048), F32),
            pltpu.VMEM((1024, 2048), BF16),
            pltpu.VMEM((1024, 128), F32),
            pltpu.VMEM((1024, 128), F32),
            pltpu.VMEM((8, 2048), F32),
            pltpu.VMEM((8, 2048), F32),
            pltpu.VMEM((1024, 128), F32),
            pltpu.VMEM((1, 2048), F32),
            pltpu.VMEM((8, BLOCK, BLOCK), F32),
            pltpu.VMEM((8, 128), F32),
            pltpu.VMEM((8, 16, 128), F32),
            pltpu.VMEM((16, 32, 128), F32),
            pltpu.VMEM((8, 8, 128), F32),
            pltpu.VMEM((16, 8, 128), F32),
            pltpu.VMEM((1024, WIDTH), F32),
            pltpu.VMEM((1024, WIDTH), F32),
            pltpu.VMEM((1024, WIDTH), BF16),
            pltpu.VMEM((1024, WIDTH), BF16),
            pltpu.VMEM((1024, WIDTH), BF16),
            pltpu.VMEM((7 * BLOCK, WIDTH), BF16),
            pltpu.VMEM((7 * BLOCK, WIDTH), BF16),
            pltpu.VMEM((1024, WIDTH), BF16),
            pltpu.SemaphoreType.DMA((160,)),
            pltpu.SemaphoreType.DMA((160,)),
            pltpu.SemaphoreType.DMA((4,)),
        ],
        compiler_params=pltpu.CompilerParams(
            collective_id=0, has_side_effects=True, vmem_limit_bytes=60 * 2**20
        ),
        cost_estimate=pl.CostEstimate(flops=16106127360, bytes_accessed=2621440, transcendentals=8388608),
    )(logit_temp, image_feat, text_feat)
    step_rows = 64
    rows = pl.BlockSpec((step_rows, WIDTH), lambda i: (i, 0))
    mean_loss, grad_image, grad_text, temp_grad = pl.pallas_call(
        finalize,
        grid=(BLOCK // step_rows,),
        out_shape=(one, shape, shape, one),
        in_specs=[smem, pl.BlockSpec((8, 128), lambda i: (0, 0)), rows, rows, rows, rows],
        out_specs=(smem, rows, rows, smem),
    )(logit_temp, totals, image_feat, text_feat, sum_image, sum_text)
    return (mean_loss[0, 0], grad_image, grad_text, temp_grad[0, 0])


def solution(mesh):
    in_specs = (P(("img", "txt"), None), P(("txt", "img"), None), P())
    out_specs = (P(), P(("img", "txt"), None), P(("txt", "img"), None), P())
    return jax.shard_map(
        on_device, mesh=mesh, in_specs=in_specs, out_specs=out_specs, check_vma=False
    )
```

```python
import functools

import jax
import jax.numpy as jnp
from jax import lax
from jax.experimental import pallas as pl
from jax.experimental.pallas import tpu as pltpu
from jax.sharding import PartitionSpec as P

PLACE = {(0, 0): 0, (0, 1): 1, (1, 0): 2, (3, 0): 3, (1, 1): 4, (3, 1): 5, (2, 0): 6, (2, 1): 7}
BLOCK = 128
HALF = 64
QUARTER = 32
WIDTH = 1280
PAIRS = 16384
GROUP = 256
LOG2E = 1.4426950408889634
LN2 = 0.6931471805599453
HIGH_SHIFT = 33.0
LOW_SHIFT = 86.0
LOW_CAP = 20.0
HIGH_LEAST = 2.0**-62
F32 = jnp.float32
BF16 = jnp.bfloat16


def exp_of(temp):
    return jnp.max(jnp.exp(jnp.full((8, 128), temp, F32)))


def mod4(v):
    return lax.rem(v + 4, 4)


class Copies:
    def __init__(self, send_sems, recv_sems):
        self.send_sems, self.recv_sems = send_sems, recv_sems
        self.table = {}
        self.settled = 0

    def start(self, name, src, dst, device):
        index = len(self.table)
        copy = pltpu.make_async_remote_copy(
            src_ref=src,
            dst_ref=dst,
            send_sem=self.send_sems.at[index],
            recv_sem=self.recv_sems.at[index],
            device_id=device,
            device_id_type=pl.DeviceIdType.MESH,
        )
        copy.start()
        self.table[name] = copy

    def arrived(self, name):
        self.table[name].wait_recv()

    def settle(self, count):
        for copy in list(self.table.values())[self.settled : count]:
            copy.wait_send()
        self.settled = count


def kernel(
    temp_ref,
    image_hbm,
    text_hbm,
    totals_ref,
    sum_image_hbm,
    sum_text_hbm,
    image_ref,
    text_ref,
    img,
    txt,
    dots,
    wts,
    row1,
    row2,
    col1,
    col2,
    row_shift,
    col_shift,
    diagonals,
    extra,
    img_stats,
    txt_stats,
    sums_a,
    sums_b,
    img_acc,
    txt_acc,
    img_out,
    txt_out,
    core_out,
    img_in,
    txt_in,
    core_in,
    send_sems,
    recv_sems,
    local_sems,
):
    img_index = lax.axis_index("img")
    txt_index = lax.axis_index("txt")
    x, core = img_index // 2, lax.rem(img_index, 2)
    y, z = txt_index // 4, lax.rem(txt_index, 4)
    odd = lax.rem(z, 2)
    z_img = z + 1 - 2 * odd
    z_txt = mod4(z - 1 + 2 * odd)

    def img_peer(r, q):
        return (img_index, mod4(y + r) * 4 + (z_img if q else z))

    def txt_peer(r, q, c=0):
        return (
            mod4(x + r) * 2 + (1 - core if c else core),
            y * 4 + (z_txt if q else z),
        )

    img_offsets = [(r, q) for r in range(4) for q in range(2) if (r, q) != (0, 0)]
    txt_offsets = [
        (r, q, c) for r in range(4) for q in range(2) for c in range(2) if (r, q, c) != (0, 0, 0)
    ]
    load_image = pltpu.make_async_copy(image_hbm, image_ref, local_sems.at[0])
    load_text = pltpu.make_async_copy(text_hbm, text_ref, local_sems.at[1])
    load_image.start()
    load_text.start()
    barrier = pltpu.get_barrier_semaphore()
    for offset in img_offsets:
        pl.semaphore_signal(barrier, inc=1, device_id=img_peer(*offset), device_id_type=pl.DeviceIdType.MESH)
    for offset in txt_offsets:
        pl.semaphore_signal(barrier, inc=1, device_id=txt_peer(*offset), device_id_type=pl.DeviceIdType.MESH)

    scale = exp_of(temp_ref[0, 0])
    slope = scale * LOG2E

    def inverse_of(rows):
        return lax.rsqrt(jnp.sum(rows * rows, axis=1, keepdims=True) + 1e-06)

    def normalize(source, target):
        for first in range(0, BLOCK, 32):
            rows = source[first : first + 32, :]
            target[first : first + 32, :] = (rows * inverse_of(rows)).astype(BF16)

    load_image.wait()
    normalize(image_ref, img)
    pl.semaphore_wait(barrier, len(img_offsets) + len(txt_offsets))

    copies = Copies(send_sems, recv_sems)

    def half(place, part):
        return pl.ds(place * BLOCK + part * HALF, HALF)

    sides = (("i", img, img_peer), ("t", txt, txt_peer))

    def push(side, name, place, first, count, to_place, r, q):
        label, rows, peer = side
        copies.start(
            label + name + str(first),
            rows.at[pl.ds(place * BLOCK + first, count)],
            rows.at[pl.ds(to_place * BLOCK + first, count)],
            peer(r, q),
        )

    def to_core(place, first, count):
        copies.start(
            "c%d_%d" % (place, first),
            txt.at[pl.ds(place * BLOCK + first, count)],
            txt.at[pl.ds((8 + place) * BLOCK + first, count)],
            txt_peer(0, 0, 1),
        )

    def push_own(side):
        push(side, "up", 0, 0, QUARTER, PLACE[3, 0], 1, 0)
        push(side, "down", 0, 64, QUARTER, PLACE[1, 0], 3, 0)
        push(side, "z", 0, 0, HALF, PLACE[0, 1], 0, 1)
        push(side, "up", 0, 32, QUARTER, PLACE[3, 0], 1, 0)
        push(side, "down", 0, 96, QUARTER, PLACE[1, 0], 3, 0)
        push(side, "up", 0, 64, HALF, PLACE[3, 0], 1, 0)
        push(side, "down", 0, 0, HALF, PLACE[1, 0], 3, 0)
        push(side, "z", 0, 64, HALF, PLACE[0, 1], 0, 1)

    push_own(sides[0])
    load_text.wait()
    normalize(text_ref, txt)
    push_own(sides[1])
    to_core(0, 0, BLOCK)

    row1[...] = jnp.zeros_like(row1)
    row2[...] = jnp.zeros_like(row2)
    col1[...] = jnp.zeros_like(col1)
    col2[...] = jnp.zeros_like(col2)

    def forward(row, row_count, column, column_count):
        cols = pl.ds(column, column_count)
        product = lax.dot_general(
            img[pl.ds(row, row_count), :],
            txt[cols, :],
            (((1,), (1,)), ((), ())),
            preferred_element_type=F32,
        )
        dots[pl.ds(row, row_count), cols] = product * slope

        for first in range(row, row + row_count, 32):
            part = pl.ds(first, 32)
            add1 = jnp.zeros((32, 128), F32)
            add2 = jnp.zeros((32, 128), F32)
            for lane in range(column, column + column_count, 128):
                block_cols = pl.ds(lane, 128)
                score = dots[part, block_cols]
                mass1 = jnp.exp2(score - HIGH_SHIFT)
                mass2 = jnp.exp2(jnp.minimum(score, LOW_CAP) + LOW_SHIFT)
                add1 = add1 + mass1
                add2 = add2 + mass2
                col1[:, block_cols] += jnp.sum(mass1.reshape(32 // 8, 8, 128), axis=0)
                col2[:, block_cols] += jnp.sum(mass2.reshape(32 // 8, 8, 128), axis=0)
            row1[part, :] += add1
            row2[part, :] += add2

    def wait_core(*names):
        for name in names:
            copies.arrived("c" + name)

    def take(name, first):
        for side in sides:
            copies.arrived(side[0] + name + str(first))

    for first in (0, 32):
        for side in sides:
            copies.arrived(side[0] + "up" + str(first))
            push(side, "up2_", PLACE[3, 0], first, QUARTER, PLACE[2, 0], 1, 0)
            copies.arrived(side[0] + "down" + str(64 + first))
            push(side, "down2_", PLACE[1, 0], 64 + first, QUARTER, PLACE[2, 0], 3, 0)
    to_core(PLACE[3, 0], 0, HALF)
    to_core(PLACE[1, 0], 64, HALF)
    take("up", 64)
    take("down", 0)
    to_core(PLACE[3, 0], 64, HALF)
    to_core(PLACE[1, 0], 0, HALF)
    for first in (0, 64):
        for side in sides:
            copies.arrived(side[0] + "z" + str(first))
            push(side, "zup", PLACE[0, 1], first, HALF, PLACE[3, 1], 1, 0)
            push(side, "zdown", PLACE[0, 1], first, HALF, PLACE[1, 1], 3, 0)
    to_core(PLACE[0, 1], 0, BLOCK)
    for first in (0, 32):
        for side in sides:
            copies.arrived(side[0] + "up2_" + str(first))
            push(side, "up2z", PLACE[2, 0], first, QUARTER, PLACE[2, 1], 0, 1)
            copies.arrived(side[0] + "down2_" + str(64 + first))
            push(side, "down2z", PLACE[2, 0], 64 + first, QUARTER, PLACE[2, 1], 0, 1)
    to_core(PLACE[2, 0], 0, BLOCK)
    forward(0, 512, 0, 512)
    wait_core("0_0", "1_0", "2_0", "2_64", "3_0", "3_64", "6_0")
    forward(0, 512, 1024, 512)
    take("zup", 0)
    take("zdown", 0)
    to_core(PLACE[3, 1], 0, HALF)
    to_core(PLACE[1, 1], 0, HALF)
    forward(768, 128, 0, 512)
    forward(768, 128, 1024, 512)
    take("up2z", 0)
    take("down2z", 64)
    take("up2z", 32)
    take("down2z", 96)
    to_core(PLACE[2, 1], 0, BLOCK)
    take("zup", 64)
    take("zdown", 64)
    to_core(PLACE[3, 1], 64, HALF)
    to_core(PLACE[1, 1], 64, HALF)
    forward(512, 256, 0, 1024)
    forward(896, 128, 0, 512)
    forward(0, 512, 512, 512)
    forward(768, 256, 512, 512)
    wait_core("7_0", "4_0", "5_0", "4_64", "5_64")
    forward(512, 256, 1024, 1024)
    forward(896, 128, 1024, 512)
    forward(0, 512, 1536, 512)
    forward(768, 256, 1536, 512)

    gather_count = len(copies.table)

    def img_order(r, q):
        return mod4(y + r) * 2 + (1 - odd if q else odd)

    def txt_order(r, q, c):
        return (mod4(x + r) * 2 + (odd if q else 1 - odd)) * 2 + (1 - core if c else core)

    for (r, q), place in PLACE.items():
        for c in range(2):
            cols = pl.ds((8 * c + place) * BLOCK, BLOCK)
            where = txt_order(r, q, c)
            txt_stats[0, pl.ds(where, 1), :] = jnp.sum(col1[:, cols], axis=0, keepdims=True)
            txt_stats[0, pl.ds(16 + where, 1), :] = jnp.sum(col2[:, cols], axis=0, keepdims=True)
    for r, q, c in txt_offsets:
        index = 8 * c + PLACE[(4 - r) % 4, q]
        copies.start("st%d" % index, txt_stats.at[0], txt_stats.at[index], txt_peer(r, q, c))
    for (r, q), place in PLACE.items():
        rows = pl.ds(place * BLOCK, BLOCK)
        where = img_order(r, q)
        img_stats[0, pl.ds(where, 1), :] = jnp.sum(row1[rows, :].T, axis=0, keepdims=True)
        img_stats[0, pl.ds(8 + where, 1), :] = jnp.sum(row2[rows, :].T, axis=0, keepdims=True)
    for r, q in img_offsets:
        index = PLACE[(4 - r) % 4, q]
        copies.start("si%d" % index, img_stats.at[0], img_stats.at[index], img_peer(r, q))

    eye = lax.broadcasted_iota(jnp.int32, (BLOCK, BLOCK), 0) == lax.broadcasted_iota(jnp.int32, (BLOCK, BLOCK), 1)

    def on_diagonal(place, body, wanted=lambda group: 1):
        r, q = [key for key in PLACE if PLACE[key] == place][0]
        y_row, z_row = mod4(y + r), (z_img if q else z)
        x_text, z_text, core_text = lax.rem(y_row, 2) * 2 + z_row // 2, 2 * core + y_row // 2, lax.rem(z_row, 2)
        near = jnp.where(z_text == z, 1, 0)
        far = jnp.where(z_text == z_txt, 1, 0)
        ring = mod4(x_text - x)
        place_text = jnp.where(
            ring == 0, far, jnp.where(ring == 1, 2 + 2 * far, jnp.where(ring == 2, 6 + far, 3 + 2 * far))
        )
        place_text = place_text + 8 * jnp.where(core_text == core, 0, 1)

        @pl.when(jnp.where(x == y, near + far, 0) * wanted(place_text // 2) == 1)
        def _():
            body(pl.ds(place * BLOCK, BLOCK), pl.ds(pl.multiple_of(place_text * BLOCK, BLOCK), BLOCK))

    for place in range(8):

        def set_aside(rows, cols, place=place):
            scores = dots[rows, cols]
            diagonals[place] = scores
            dots[rows, cols] = jnp.where(eye, -10000.0, scores)

        on_diagonal(place, set_aside)

    def log_sum(high, low):
        return jnp.where(
            high >= HIGH_LEAST,
            jnp.log(high) * LOG2E + HIGH_SHIFT,
            jnp.log(jnp.maximum(low, 1e-37)) * LOG2E - LOW_SHIFT,
        )

    copies.settle(gather_count)
    img_total = img_stats[0]
    for index in range(1, 8):
        copies.arrived("si%d" % index)
        img_total = img_total + img_stats[index]
    row_lse = log_sum(img_total[:8], img_total[8:])
    row1[0:8, :] = row_lse
    own_lse = row1[pl.ds(img_order(0, 0), 1), :]
    for (r, q), place in PLACE.items():
        one = row1[pl.ds(img_order(r, q), 1), :]
        row_shift[pl.ds(place * BLOCK, BLOCK), :] = jnp.broadcast_to(one + 1.0, (BLOCK, BLOCK)).T
    txt_total = txt_stats[0]
    for index in range(1, 16):
        copies.arrived("st%d" % index)
        txt_total = txt_total + txt_stats[index]
    col_lse = log_sum(txt_total[:16], txt_total[16:])
    row2[0:16, :] = col_lse
    own_lse = own_lse + row2[pl.ds(txt_order(0, 0, 0), 1), :]
    for (r, q), place in PLACE.items():
        for c in range(2):
            one = row2[pl.ds(txt_order(r, q, c), 1), :]
            col_shift[:, pl.ds((8 * c + place) * BLOCK, BLOCK)] = one + 1.0

    extra[...] = jnp.zeros_like(extra)
    heats = [jnp.zeros((16, 128), F32)] * 4

    def weigh(places, blocks):
        for place in places:
            for first in range(place * BLOCK, place * BLOCK + BLOCK, 16):
                part = pl.ds(first, 16)
                shift = row_shift[part, :]
                for block in blocks:
                    cols = pl.ds(block * BLOCK, BLOCK)
                    score = dots[part, cols]
                    weight = jnp.exp2(score - shift) + jnp.exp2(score - col_shift[:, cols])
                    heats[block % 4] = heats[block % 4] + weight * score
                    wts[part, cols] = weight.astype(BF16)

    def put_back(places, wanted):
        def body(place, rows, cols):
            scores = diagonals[place]
            weight = jnp.exp2(scores - row_shift[rows, :]) + jnp.exp2(scores - col_shift[:, cols])
            weight = jnp.where(eye, weight - 1.0, weight)
            wts[rows, cols] = weight.astype(BF16)
            extra[0:1, :] += jnp.sum(jnp.where(eye, scores, 0.0), axis=0, keepdims=True)
            extra[1:2, :] += jnp.sum(jnp.where(eye, weight * scores, 0.0), axis=0, keepdims=True)

        for place in places:
            on_diagonal(place, functools.partial(body, place), wanted)

    def block(place):
        return pl.ds(place * BLOCK, BLOCK)

    def rows_of(group):
        return pl.ds(group * GROUP, GROUP)

    def image_term(group):
        return jnp.dot(wts[rows_of(group), :], txt[...], preferred_element_type=F32)

    def text_term(group):
        return lax.dot_general(
            wts[:, rows_of(group)], img[...], (((0,), (0,)), ((), ())), preferred_element_type=F32
        )

    def core_step(group):
        rows = rows_of(group)
        core_out[rows, :] = text_term(4 + group).astype(BF16)
        copies.start("k%d" % group, core_out.at[rows], core_in.at[rows], txt_peer(0, 0, 1))

    def text_group(group):
        term = text_term(group)
        copies.arrived("k%d" % group)
        return term + core_in[rows_of(group), :].astype(F32)

    trees = (("i", img_acc, img_out, img_in, img_peer), ("t", txt_acc, txt_out, txt_in, txt_peer))

    def group_term(tree, group):
        return image_term(group) if tree[0] == "i" else text_group(group)

    def send(tree, name, place, first, count, to_place, r, q):
        label, acc, out, landing, peer = tree
        rows = pl.ds(place * BLOCK + first, count)
        copies.start(label + name, out.at[rows], landing.at[pl.ds(to_place * BLOCK + first, count)], peer(r, q))

    def lower(tree, place, first, count, slots):
        label, acc, out, landing, peer = tree
        rows = pl.ds(place * BLOCK + first, count)
        total = acc[rows, :]
        for slot in slots:
            total = total + landing[pl.ds(slot * BLOCK + first, count), :].astype(F32)
        out[rows, :] = total.astype(BF16)

    def ring_step(tree):
        tree[2][rows_of(2), :] = group_term(tree, 2).astype(BF16)
        for first in (0, HALF):
            send(tree, "zup_g%d" % first, 4, first, HALF, 1, 1, 0)
            send(tree, "zdown_g%d" % first, 5, first, HALF, 2, 3, 0)

    def far_step(tree):
        term = group_term(tree, 3)
        tree[1][block(6), :] = term[:BLOCK]
        tree[2][block(7), :] = term[BLOCK:].astype(BF16)
        for first in (0, 64, 32, 96):
            send(tree, "far_g%d" % first, 7, first, QUARTER, 0, 0, 1)

    def turn_step(tree, first):
        copies.arrived(tree[0] + "far_g%d" % first)
        lower(tree, 6, first, QUARTER, (0,))
        send(tree, "down2_g%d" % first, 6, first, QUARTER, 3, 3, 0)
        copies.arrived(tree[0] + "far_g%d" % (64 + first))
        lower(tree, 6, 64 + first, QUARTER, (0,))
        send(tree, "up2_g%d" % first, 6, 64 + first, QUARTER, 3, 1, 0)

    def free_step(tree):
        term = group_term(tree, 1)
        tree[2][half(2, 0), :] = term[:HALF].astype(BF16)
        tree[1][half(2, 1), :] = term[HALF : 2 * HALF]
        tree[1][half(3, 0), :] = term[2 * HALF : 3 * HALF]
        tree[2][half(3, 1), :] = term[3 * HALF :].astype(BF16)
        send(tree, "up_free", 2, 0, HALF, 4, 1, 0)
        send(tree, "down_free", 3, HALF, HALF, 5, 3, 0)

    def own_step(tree):
        tree[1][rows_of(0), :] = group_term(tree, 0)

    def pair_step(tree, first):
        copies.arrived(tree[0] + "zup_g%d" % first)
        copies.arrived(tree[0] + "zdown_g%d" % first)
        lower(tree, 1, first, HALF, (1, 2))
        send(tree, "z_g%d" % first, 1, first, HALF, 6, 0, 1)

    def last_step(tree, first):
        copies.arrived(tree[0] + "up2_g%d" % first)
        lower(tree, 2, 64 + first, QUARTER, (3,))
        send(tree, "up_last%d" % first, 2, 64 + first, QUARTER, 4, 1, 0)
        copies.arrived(tree[0] + "down2_g%d" % first)
        lower(tree, 3, first, QUARTER, (3,))
        send(tree, "down_last%d" % first, 3, first, QUARTER, 5, 3, 0)

    image_tree, text_tree = trees
    weigh(range(8), range(16))
    put_back(range(8), lambda group: 1)
    sums_a[0, 0:1, :] = own_lse - 2.0 * extra[0:1, :]
    sums_a[0, 1:2, :] = jnp.sum(heats[0] + heats[1] + heats[2] + heats[3], axis=0, keepdims=True) + extra[1:2, :]
    sums_a[0, 2:8, :] = jnp.zeros((6, 128), F32)
    for r, q in img_offsets:
        index = PLACE[(4 - r) % 4, q]
        copies.start("ai%d" % index, sums_a.at[0], sums_a.at[index], img_peer(r, q))

    core_step(2)
    ring_step(image_tree)
    ring_step(text_tree)
    core_step(3)
    far_step(image_tree)
    far_step(text_tree)
    core_step(1)
    free_step(image_tree)
    free_step(text_tree)
    far_count = len(copies.table)
    for index in range(1, 8):
        copies.arrived("ai%d" % index)
    total = sums_a[0]
    for index in range(1, 8):
        total = total + sums_a[index]
    sums_b[0] = total
    for r, q, c in txt_offsets:
        index = 8 * c + PLACE[(4 - r) % 4, q]
        copies.start("at%d" % index, sums_b.at[0], sums_b.at[index], txt_peer(r, q, c))
    core_step(0)
    own_step(image_tree)
    turn_step(image_tree, 0)
    own_step(text_tree)
    turn_step(text_tree, 0)
    pair_step(image_tree, 0)
    pair_step(image_tree, HALF)
    turn_step(image_tree, QUARTER)
    pair_step(text_tree, 0)
    pair_step(text_tree, HALF)
    turn_step(text_tree, QUARTER)
    for tree in trees:
        last_step(tree, 0)
    copies.settle(far_count)
    for tree in trees:
        last_step(tree, QUARTER)
    for index in range(1, 16):
        copies.arrived("at%d" % index)
    total = sums_b[0]
    for index in range(1, 16):
        total = total + sums_b[index]
    totals_ref[...] = total
    stores = []
    for tree, source, result in ((image_tree, image_ref, sum_image_hbm), (text_tree, text_ref, sum_text_hbm)):
        label, acc, out, landing, peer = tree
        for name in ("up_free", "down_free", "z_g0", "z_g64", "up_last0", "down_last0", "up_last32", "down_last32"):
            copies.arrived(label + name)
        grad = acc[block(0), :]
        for slot in (4, 5, 6):
            grad = grad + landing[block(slot), :].astype(F32)
        source[...] = grad
        stores.append(pltpu.make_async_copy(source, result, local_sems.at[2 + len(stores)]))
        stores[-1].start()
    copies.settle(len(copies.table))
    for store in stores:
        store.wait()


def finalize(
    temp_ref,
    totals_ref,
    image_ref,
    text_ref,
    sum_image_ref,
    sum_text_ref,
    loss_ref,
    grad_image_ref,
    grad_text_ref,
    temp_grad_ref,
):
    scale = exp_of(temp_ref[0, 0])
    for source, total, result in (
        (image_ref, sum_image_ref, grad_image_ref),
        (text_ref, sum_text_ref, grad_text_ref),
    ):
        rows = source[...]
        inverse = lax.rsqrt(jnp.sum(rows * rows, axis=1, keepdims=True) + 1e-06)
        grad = total[...] * scale
        unit = rows * inverse
        result[...] = inverse * (grad - unit * jnp.sum(unit * grad, axis=1, keepdims=True))
    totals = totals_ref[...]
    loss_ref[0, 0] = jnp.sum(totals[0:1, :]) * (LN2 / (2.0 * PAIRS))
    temp_grad_ref[0, 0] = jnp.sum(totals[1:2, :]) * (LN2 / PAIRS)


def on_device(image_feat, text_feat, logit_temp):
    logit_temp = logit_temp.reshape(1, 1)
    smem = pl.BlockSpec(memory_space=pltpu.SMEM)
    anywhere = pl.BlockSpec(memory_space=pl.ANY)
    one = jax.ShapeDtypeStruct((1, 1), F32)
    shape = jax.ShapeDtypeStruct((BLOCK, WIDTH), F32)
    totals, sum_image, sum_text = pl.pallas_call(
        kernel,
        out_shape=(jax.ShapeDtypeStruct((8, 128), F32), shape, shape),
        in_specs=[smem, anywhere, anywhere],
        out_specs=(pl.BlockSpec(memory_space=pltpu.VMEM), anywhere, anywhere),
        scratch_shapes=[
            pltpu.VMEM((BLOCK, WIDTH), F32),
            pltpu.VMEM((BLOCK, WIDTH), F32),
            pltpu.VMEM((1024, WIDTH), BF16),
            pltpu.VMEM((2048, WIDTH), BF16),
            pltpu.VMEM((1024, 2048), F32),
            pltpu.VMEM((1024, 2048), BF16),
            pltpu.VMEM((1024, 128), F32),
            pltpu.VMEM((1024, 128), F32),
            pltpu.VMEM((8, 2048), F32),
            pltpu.VMEM((8, 2048), F32),
            pltpu.VMEM((1024, 128), F32),
            pltpu.VMEM((1, 2048), F32),
            pltpu.VMEM((8, BLOCK, BLOCK), F32),
            pltpu.VMEM((8, 128), F32),
            pltpu.VMEM((8, 16, 128), F32),
            pltpu.VMEM((16, 32, 128), F32),
            pltpu.VMEM((8, 8, 128), F32),
            pltpu.VMEM((16, 8, 128), F32),
            pltpu.VMEM((1024, WIDTH), F32),
            pltpu.VMEM((1024, WIDTH), F32),
            pltpu.VMEM((1024, WIDTH), BF16),
            pltpu.VMEM((1024, WIDTH), BF16),
            pltpu.VMEM((1024, WIDTH), BF16),
            pltpu.VMEM((7 * BLOCK, WIDTH), BF16),
            pltpu.VMEM((7 * BLOCK, WIDTH), BF16),
            pltpu.VMEM((1024, WIDTH), BF16),
            pltpu.SemaphoreType.DMA((160,)),
            pltpu.SemaphoreType.DMA((160,)),
            pltpu.SemaphoreType.DMA((4,)),
        ],
        compiler_params=pltpu.CompilerParams(
            collective_id=0, has_side_effects=True, vmem_limit_bytes=60 * 2**20
        ),
        cost_estimate=pl.CostEstimate(flops=16106127360, bytes_accessed=2621440, transcendentals=8388608),
    )(logit_temp, image_feat, text_feat)
    step_rows = 64
    rows = pl.BlockSpec((step_rows, WIDTH), lambda i: (i, 0))
    mean_loss, grad_image, grad_text, temp_grad = pl.pallas_call(
        finalize,
        grid=(BLOCK // step_rows,),
        out_shape=(one, shape, shape, one),
        in_specs=[smem, pl.BlockSpec((8, 128), lambda i: (0, 0)), rows, rows, rows, rows],
        out_specs=(smem, rows, rows, smem),
    )(logit_temp, totals, image_feat, text_feat, sum_image, sum_text)
    return (mean_loss[0, 0], grad_image, grad_text, temp_grad[0, 0])


def solution(mesh):
    in_specs = (P(("img", "txt"), None), P(("txt", "img"), None), P())
    out_specs = (P(), P(("img", "txt"), None), P(("txt", "img"), None), P())
    return jax.shard_map(
        on_device, mesh=mesh, in_specs=in_specs, out_specs=out_specs, check_vma=False
    )
```

```python
import functools

import jax
import jax.numpy as jnp
from jax import lax
from jax.experimental import pallas as pl
from jax.experimental.pallas import tpu as pltpu
from jax.sharding import PartitionSpec as P

PLACE = {(0, 0): 0, (0, 1): 1, (1, 0): 2, (3, 0): 3, (1, 1): 4, (3, 1): 5, (2, 0): 6, (2, 1): 7}
BLOCK = 128
HALF = 64
QUARTER = 32
WIDTH = 1280
PAIRS = 16384
GROUP = 256
LOG2E = 1.4426950408889634
LN2 = 0.6931471805599453
HIGH_SHIFT = 33.0
LOW_SHIFT = 86.0
LOW_CAP = 20.0
HIGH_LEAST = 2.0**-62
F32 = jnp.float32
BF16 = jnp.bfloat16


def exp_of(temp):
    return jnp.max(jnp.exp(jnp.full((8, 128), temp, F32)))


def mod4(v):
    return lax.rem(v + 4, 4)


class Copies:
    def __init__(self, send_sems, recv_sems):
        self.send_sems, self.recv_sems = send_sems, recv_sems
        self.table = {}
        self.settled = 0

    def start(self, name, src, dst, device):
        index = len(self.table)
        copy = pltpu.make_async_remote_copy(
            src_ref=src,
            dst_ref=dst,
            send_sem=self.send_sems.at[index],
            recv_sem=self.recv_sems.at[index],
            device_id=device,
            device_id_type=pl.DeviceIdType.MESH,
        )
        copy.start()
        self.table[name] = copy

    def arrived(self, name):
        self.table[name].wait_recv()

    def settle(self, count):
        for copy in list(self.table.values())[self.settled : count]:
            copy.wait_send()
        self.settled = count


def kernel(
    temp_ref,
    image_hbm,
    text_hbm,
    totals_ref,
    sum_image_hbm,
    sum_text_hbm,
    image_ref,
    text_ref,
    img,
    txt,
    dots,
    wts,
    row1,
    row2,
    col1,
    col2,
    row_shift,
    col_shift,
    diagonals,
    extra,
    img_stats,
    txt_stats,
    sums_a,
    sums_b,
    img_acc,
    txt_acc,
    img_out,
    txt_out,
    core_out,
    img_in,
    txt_in,
    core_in,
    send_sems,
    recv_sems,
    local_sems,
):
    img_index = lax.axis_index("img")
    txt_index = lax.axis_index("txt")
    x, core = img_index // 2, lax.rem(img_index, 2)
    y, z = txt_index // 4, lax.rem(txt_index, 4)
    odd = lax.rem(z, 2)
    z_img = z + 1 - 2 * odd
    z_txt = mod4(z - 1 + 2 * odd)

    def img_peer(r, q):
        return (img_index, mod4(y + r) * 4 + (z_img if q else z))

    def txt_peer(r, q, c=0):
        return (
            mod4(x + r) * 2 + (1 - core if c else core),
            y * 4 + (z_txt if q else z),
        )

    img_offsets = [(r, q) for r in range(4) for q in range(2) if (r, q) != (0, 0)]
    txt_offsets = [
        (r, q, c) for r in range(4) for q in range(2) for c in range(2) if (r, q, c) != (0, 0, 0)
    ]
    load_image = pltpu.make_async_copy(image_hbm, image_ref, local_sems.at[0])
    load_text = pltpu.make_async_copy(text_hbm, text_ref, local_sems.at[1])
    load_image.start()
    load_text.start()
    barrier = pltpu.get_barrier_semaphore()
    for offset in img_offsets:
        pl.semaphore_signal(barrier, inc=1, device_id=img_peer(*offset), device_id_type=pl.DeviceIdType.MESH)
    for offset in txt_offsets:
        pl.semaphore_signal(barrier, inc=1, device_id=txt_peer(*offset), device_id_type=pl.DeviceIdType.MESH)

    scale = exp_of(temp_ref[0, 0])
    slope = scale * LOG2E

    def inverse_of(rows):
        return lax.rsqrt(jnp.sum(rows * rows, axis=1, keepdims=True) + 1e-06)

    def normalize(source, target):
        for first in range(0, BLOCK, 32):
            rows = source[first : first + 32, :]
            target[first : first + 32, :] = (rows * inverse_of(rows)).astype(BF16)

    load_image.wait()
    normalize(image_ref, img)
    pl.semaphore_wait(barrier, len(img_offsets) + len(txt_offsets))

    copies = Copies(send_sems, recv_sems)

    def half(place, part):
        return pl.ds(place * BLOCK + part * HALF, HALF)

    sides = (("i", img, img_peer), ("t", txt, txt_peer))

    def push(side, name, place, first, count, to_place, r, q):
        label, rows, peer = side
        copies.start(
            label + name + str(first),
            rows.at[pl.ds(place * BLOCK + first, count)],
            rows.at[pl.ds(to_place * BLOCK + first, count)],
            peer(r, q),
        )

    def to_core(place, first, count):
        copies.start(
            "c%d_%d" % (place, first),
            txt.at[pl.ds(place * BLOCK + first, count)],
            txt.at[pl.ds((8 + place) * BLOCK + first, count)],
            txt_peer(0, 0, 1),
        )

    def push_own(side):
        push(side, "up", 0, 0, QUARTER, PLACE[3, 0], 1, 0)
        push(side, "down", 0, 64, QUARTER, PLACE[1, 0], 3, 0)
        push(side, "z", 0, 0, HALF, PLACE[0, 1], 0, 1)
        push(side, "up", 0, 32, QUARTER, PLACE[3, 0], 1, 0)
        push(side, "down", 0, 96, QUARTER, PLACE[1, 0], 3, 0)
        push(side, "up", 0, 64, HALF, PLACE[3, 0], 1, 0)
        push(side, "down", 0, 0, HALF, PLACE[1, 0], 3, 0)
        push(side, "z", 0, 64, HALF, PLACE[0, 1], 0, 1)

    push_own(sides[0])
    load_text.wait()
    normalize(text_ref, txt)
    push_own(sides[1])
    to_core(0, 0, BLOCK)

    row1[...] = jnp.zeros_like(row1)
    row2[...] = jnp.zeros_like(row2)
    col1[...] = jnp.zeros_like(col1)
    col2[...] = jnp.zeros_like(col2)

    def forward(row, row_count, column, column_count):
        cols = pl.ds(column, column_count)
        product = lax.dot_general(
            img[pl.ds(row, row_count), :],
            txt[cols, :],
            (((1,), (1,)), ((), ())),
            preferred_element_type=F32,
        )
        dots[pl.ds(row, row_count), cols] = product * slope

        for first in range(row, row + row_count, 32):
            part = pl.ds(first, 32)
            add1 = jnp.zeros((32, 128), F32)
            add2 = jnp.zeros((32, 128), F32)
            for lane in range(column, column + column_count, 128):
                block_cols = pl.ds(lane, 128)
                score = dots[part, block_cols]
                mass1 = jnp.exp2(score - HIGH_SHIFT)
                mass2 = jnp.exp2(jnp.minimum(score, LOW_CAP) + LOW_SHIFT)
                add1 = add1 + mass1
                add2 = add2 + mass2
                col1[:, block_cols] += jnp.sum(mass1.reshape(32 // 8, 8, 128), axis=0)
                col2[:, block_cols] += jnp.sum(mass2.reshape(32 // 8, 8, 128), axis=0)
            row1[part, :] += add1
            row2[part, :] += add2

    def wait_core(*names):
        for name in names:
            copies.arrived("c" + name)

    def take(name, first):
        for side in sides:
            copies.arrived(side[0] + name + str(first))

    for first in (0, 32):
        for side in sides:
            copies.arrived(side[0] + "up" + str(first))
            push(side, "up2_", PLACE[3, 0], first, QUARTER, PLACE[2, 0], 1, 0)
            copies.arrived(side[0] + "down" + str(64 + first))
            push(side, "down2_", PLACE[1, 0], 64 + first, QUARTER, PLACE[2, 0], 3, 0)
            if first == 32:
                push(side, "zup", PLACE[3, 0], 32, 16, PLACE[3, 1], 0, 1)
                push(side, "zdown", PLACE[1, 0], 96, 16, PLACE[1, 1], 0, 1)
    to_core(PLACE[3, 0], 0, HALF)
    to_core(PLACE[1, 0], 64, HALF)
    take("up", 64)
    take("down", 0)
    to_core(PLACE[3, 0], 64, HALF)
    to_core(PLACE[1, 0], 0, HALF)
    for first in (0, 64):
        for side in sides:
            copies.arrived(side[0] + "z" + str(first))
            if first == 0:
                push(side, "zup", PLACE[0, 1], 0, 32, PLACE[3, 1], 1, 0)
                push(side, "zdown", PLACE[0, 1], 0, 64, PLACE[1, 1], 3, 0)
            else:
                push(side, "zup", PLACE[0, 1], 48, 80, PLACE[3, 1], 1, 0)
                push(side, "zdown", PLACE[0, 1], 64, 32, PLACE[1, 1], 3, 0)
                push(side, "zdown", PLACE[0, 1], 112, 16, PLACE[1, 1], 3, 0)
    to_core(PLACE[0, 1], 0, BLOCK)
    for first in (0, 32):
        for side in sides:
            copies.arrived(side[0] + "up2_" + str(first))
            push(side, "up2z", PLACE[2, 0], first, QUARTER, PLACE[2, 1], 0, 1)
            copies.arrived(side[0] + "down2_" + str(64 + first))
            push(side, "down2z", PLACE[2, 0], 64 + first, QUARTER, PLACE[2, 1], 0, 1)
    to_core(PLACE[2, 0], 0, BLOCK)
    forward(0, 512, 0, 512)
    wait_core("0_0", "1_0", "2_0", "2_64", "3_0", "3_64", "6_0")
    forward(0, 512, 1024, 512)
    take("zup", 0)
    take("zdown", 0)
    take("zup", 32)
    take("zdown", 96)
    to_core(PLACE[3, 1], 0, 48)
    to_core(PLACE[1, 1], 0, HALF)
    forward(768, 128, 0, 512)
    forward(768, 128, 1024, 512)
    take("up2z", 0)
    take("down2z", 64)
    take("up2z", 32)
    take("down2z", 96)
    to_core(PLACE[2, 1], 0, BLOCK)
    take("zup", 48)
    take("zdown", 64)
    take("zdown", 112)
    to_core(PLACE[3, 1], 48, 80)
    to_core(PLACE[1, 1], 64, HALF)
    forward(512, 256, 0, 1024)
    forward(896, 128, 0, 512)
    forward(0, 512, 512, 512)
    forward(768, 256, 512, 512)
    wait_core("7_0", "4_0", "5_0", "4_64", "5_48")
    forward(512, 256, 1024, 1024)
    forward(896, 128, 1024, 512)
    forward(0, 512, 1536, 512)
    forward(768, 256, 1536, 512)

    gather_count = len(copies.table)

    def img_order(r, q):
        return mod4(y + r) * 2 + (1 - odd if q else odd)

    def txt_order(r, q, c):
        return (mod4(x + r) * 2 + (odd if q else 1 - odd)) * 2 + (1 - core if c else core)

    for (r, q), place in PLACE.items():
        for c in range(2):
            cols = pl.ds((8 * c + place) * BLOCK, BLOCK)
            where = txt_order(r, q, c)
            txt_stats[0, pl.ds(where, 1), :] = jnp.sum(col1[:, cols], axis=0, keepdims=True)
            txt_stats[0, pl.ds(16 + where, 1), :] = jnp.sum(col2[:, cols], axis=0, keepdims=True)
    for r, q, c in txt_offsets:
        index = 8 * c + PLACE[(4 - r) % 4, q]
        copies.start("st%d" % index, txt_stats.at[0], txt_stats.at[index], txt_peer(r, q, c))
    for (r, q), place in PLACE.items():
        rows = pl.ds(place * BLOCK, BLOCK)
        where = img_order(r, q)
        img_stats[0, pl.ds(where, 1), :] = jnp.sum(row1[rows, :].T, axis=0, keepdims=True)
        img_stats[0, pl.ds(8 + where, 1), :] = jnp.sum(row2[rows, :].T, axis=0, keepdims=True)
    for r, q in img_offsets:
        index = PLACE[(4 - r) % 4, q]
        copies.start("si%d" % index, img_stats.at[0], img_stats.at[index], img_peer(r, q))

    eye = lax.broadcasted_iota(jnp.int32, (BLOCK, BLOCK), 0) == lax.broadcasted_iota(jnp.int32, (BLOCK, BLOCK), 1)

    def on_diagonal(place, body, wanted=lambda group: 1):
        r, q = [key for key in PLACE if PLACE[key] == place][0]
        y_row, z_row = mod4(y + r), (z_img if q else z)
        x_text, z_text, core_text = lax.rem(y_row, 2) * 2 + z_row // 2, 2 * core + y_row // 2, lax.rem(z_row, 2)
        near = jnp.where(z_text == z, 1, 0)
        far = jnp.where(z_text == z_txt, 1, 0)
        ring = mod4(x_text - x)
        place_text = jnp.where(
            ring == 0, far, jnp.where(ring == 1, 2 + 2 * far, jnp.where(ring == 2, 6 + far, 3 + 2 * far))
        )
        place_text = place_text + 8 * jnp.where(core_text == core, 0, 1)

        @pl.when(jnp.where(x == y, near + far, 0) * wanted(place_text // 2) == 1)
        def _():
            body(pl.ds(place * BLOCK, BLOCK), pl.ds(pl.multiple_of(place_text * BLOCK, BLOCK), BLOCK))

    for place in range(8):

        def set_aside(rows, cols, place=place):
            scores = dots[rows, cols]
            diagonals[place] = scores
            dots[rows, cols] = jnp.where(eye, -10000.0, scores)

        on_diagonal(place, set_aside)

    def log_sum(high, low):
        return jnp.where(
            high >= HIGH_LEAST,
            jnp.log(high) * LOG2E + HIGH_SHIFT,
            jnp.log(jnp.maximum(low, 1e-37)) * LOG2E - LOW_SHIFT,
        )

    copies.settle(gather_count)
    img_total = img_stats[0]
    for index in range(1, 8):
        copies.arrived("si%d" % index)
        img_total = img_total + img_stats[index]
    row_lse = log_sum(img_total[:8], img_total[8:])
    row1[0:8, :] = row_lse
    own_lse = row1[pl.ds(img_order(0, 0), 1), :]
    for (r, q), place in PLACE.items():
        one = row1[pl.ds(img_order(r, q), 1), :]
        row_shift[pl.ds(place * BLOCK, BLOCK), :] = jnp.broadcast_to(one + 1.0, (BLOCK, BLOCK)).T
    txt_total = txt_stats[0]
    for index in range(1, 16):
        copies.arrived("st%d" % index)
        txt_total = txt_total + txt_stats[index]
    col_lse = log_sum(txt_total[:16], txt_total[16:])
    row2[0:16, :] = col_lse
    own_lse = own_lse + row2[pl.ds(txt_order(0, 0, 0), 1), :]
    for (r, q), place in PLACE.items():
        for c in range(2):
            one = row2[pl.ds(txt_order(r, q, c), 1), :]
            col_shift[:, pl.ds((8 * c + place) * BLOCK, BLOCK)] = one + 1.0

    extra[...] = jnp.zeros_like(extra)
    heats = [jnp.zeros((16, 128), F32)] * 4

    def weigh(places, blocks):
        for place in places:
            for first in range(place * BLOCK, place * BLOCK + BLOCK, 16):
                part = pl.ds(first, 16)
                shift = row_shift[part, :]
                for block in blocks:
                    cols = pl.ds(block * BLOCK, BLOCK)
                    score = dots[part, cols]
                    weight = jnp.exp2(score - shift) + jnp.exp2(score - col_shift[:, cols])
                    heats[block % 4] = heats[block % 4] + weight * score
                    wts[part, cols] = weight.astype(BF16)

    def put_back(places, wanted):
        def body(place, rows, cols):
            scores = diagonals[place]
            weight = jnp.exp2(scores - row_shift[rows, :]) + jnp.exp2(scores - col_shift[:, cols])
            weight = jnp.where(eye, weight - 1.0, weight)
            wts[rows, cols] = weight.astype(BF16)
            extra[0:1, :] += jnp.sum(jnp.where(eye, scores, 0.0), axis=0, keepdims=True)
            extra[1:2, :] += jnp.sum(jnp.where(eye, weight * scores, 0.0), axis=0, keepdims=True)

        for place in places:
            on_diagonal(place, functools.partial(body, place), wanted)

    def block(place):
        return pl.ds(place * BLOCK, BLOCK)

    def rows_of(group):
        return pl.ds(group * GROUP, GROUP)

    def image_term(group):
        return jnp.dot(wts[rows_of(group), :], txt[...], preferred_element_type=F32)

    def text_term(group):
        return lax.dot_general(
            wts[:, rows_of(group)], img[...], (((0,), (0,)), ((), ())), preferred_element_type=F32
        )

    def core_step(group):
        rows = rows_of(group)
        core_out[rows, :] = text_term(4 + group).astype(BF16)
        copies.start("k%d" % group, core_out.at[rows], core_in.at[rows], txt_peer(0, 0, 1))

    def text_group(group):
        term = text_term(group)
        copies.arrived("k%d" % group)
        return term + core_in[rows_of(group), :].astype(F32)

    trees = (("i", img_acc, img_out, img_in, img_peer), ("t", txt_acc, txt_out, txt_in, txt_peer))

    def group_term(tree, group):
        return image_term(group) if tree[0] == "i" else text_group(group)

    def send(tree, name, place, first, count, to_place, r, q):
        label, acc, out, landing, peer = tree
        rows = pl.ds(place * BLOCK + first, count)
        copies.start(label + name, out.at[rows], landing.at[pl.ds(to_place * BLOCK + first, count)], peer(r, q))

    def lower(tree, place, first, count, slots):
        label, acc, out, landing, peer = tree
        rows = pl.ds(place * BLOCK + first, count)
        total = acc[rows, :]
        for slot in slots:
            total = total + landing[pl.ds(slot * BLOCK + first, count), :].astype(F32)
        out[rows, :] = total.astype(BF16)

    def ring_step(tree):
        tree[2][rows_of(2), :] = group_term(tree, 2).astype(BF16)
        for first in (0, HALF):
            send(tree, "zup_g%d" % first, 4, first, HALF, 1, 1, 0)
            send(tree, "zdown_g%d" % first, 5, first, HALF, 2, 3, 0)

    def far_step(tree):
        term = group_term(tree, 3)
        tree[1][block(6), :] = term[:BLOCK]
        tree[2][block(7), :] = term[BLOCK:].astype(BF16)
        for first in (0, 64, 32, 96):
            send(tree, "far_g%d" % first, 7, first, QUARTER, 0, 0, 1)

    def turn_step(tree, first):
        copies.arrived(tree[0] + "far_g%d" % first)
        lower(tree, 6, first, QUARTER, (0,))
        send(tree, "down2_g%d" % first, 6, first, QUARTER, 3, 3, 0)
        copies.arrived(tree[0] + "far_g%d" % (64 + first))
        lower(tree, 6, 64 + first, QUARTER, (0,))
        send(tree, "up2_g%d" % first, 6, 64 + first, QUARTER, 3, 1, 0)

    def free_step(tree):
        term = group_term(tree, 1)
        tree[2][half(2, 0), :] = term[:HALF].astype(BF16)
        tree[1][half(2, 1), :] = term[HALF : 2 * HALF]
        tree[1][half(3, 0), :] = term[2 * HALF : 3 * HALF]
        tree[2][half(3, 1), :] = term[3 * HALF :].astype(BF16)
        send(tree, "up_free", 2, 0, HALF, 4, 1, 0)
        send(tree, "down_free", 3, HALF, HALF, 5, 3, 0)

    def own_step(tree):
        tree[1][rows_of(0), :] = group_term(tree, 0)

    def pair_step(tree, first):
        copies.arrived(tree[0] + "zup_g%d" % first)
        copies.arrived(tree[0] + "zdown_g%d" % first)
        lower(tree, 1, first, HALF, (1, 2))
        send(tree, "z_g%d" % first, 1, first, HALF, 6, 0, 1)

    def last_step(tree, first):
        copies.arrived(tree[0] + "up2_g%d" % first)
        lower(tree, 2, 64 + first, QUARTER, (3,))
        send(tree, "up_last%d" % first, 2, 64 + first, QUARTER, 4, 1, 0)
        copies.arrived(tree[0] + "down2_g%d" % first)
        lower(tree, 3, first, QUARTER, (3,))
        send(tree, "down_last%d" % first, 3, first, QUARTER, 5, 3, 0)

    image_tree, text_tree = trees
    weigh(range(8), range(16))
    put_back(range(8), lambda group: 1)
    sums_a[0, 0:1, :] = own_lse - 2.0 * extra[0:1, :]
    sums_a[0, 1:2, :] = jnp.sum(heats[0] + heats[1] + heats[2] + heats[3], axis=0, keepdims=True) + extra[1:2, :]
    sums_a[0, 2:8, :] = jnp.zeros((6, 128), F32)
    for r, q in img_offsets:
        index = PLACE[(4 - r) % 4, q]
        copies.start("ai%d" % index, sums_a.at[0], sums_a.at[index], img_peer(r, q))

    core_step(2)
    ring_step(image_tree)
    ring_step(text_tree)
    core_step(3)
    far_step(image_tree)
    far_step(text_tree)
    core_step(1)
    free_step(image_tree)
    free_step(text_tree)
    far_count = len(copies.table)
    for index in range(1, 8):
        copies.arrived("ai%d" % index)
    total = sums_a[0]
    for index in range(1, 8):
        total = total + sums_a[index]
    sums_b[0] = total
    for r, q, c in txt_offsets:
        index = 8 * c + PLACE[(4 - r) % 4, q]
        copies.start("at%d" % index, sums_b.at[0], sums_b.at[index], txt_peer(r, q, c))
    core_step(0)
    own_step(image_tree)
    turn_step(image_tree, 0)
    own_step(text_tree)
    turn_step(text_tree, 0)
    pair_step(image_tree, 0)
    pair_step(image_tree, HALF)
    turn_step(image_tree, QUARTER)
    pair_step(text_tree, 0)
    pair_step(text_tree, HALF)
    turn_step(text_tree, QUARTER)
    for tree in trees:
        last_step(tree, 0)
    copies.settle(far_count)
    for tree in trees:
        last_step(tree, QUARTER)
    for index in range(1, 16):
        copies.arrived("at%d" % index)
    total = sums_b[0]
    for index in range(1, 16):
        total = total + sums_b[index]
    totals_ref[...] = total
    stores = []
    for tree, result in ((image_tree, sum_image_hbm), (text_tree, sum_text_hbm)):
        label, acc, out, landing, peer = tree
        for name in ("up_free", "down_free", "z_g0", "z_g64", "up_last0", "down_last0", "up_last32", "down_last32"):
            copies.arrived(label + name)
        grad = acc[block(0), :]
        for slot in (4, 5, 6):
            grad = grad + landing[block(slot), :].astype(F32)
        out[block(0), :] = grad.astype(BF16)
        stores.append(pltpu.make_async_copy(out.at[block(0)], result, local_sems.at[2 + len(stores)]))
        stores[-1].start()
    copies.settle(len(copies.table))
    for store in stores:
        store.wait()


def finalize(
    temp_ref,
    totals_ref,
    image_ref,
    text_ref,
    sum_image_ref,
    sum_text_ref,
    loss_ref,
    grad_image_ref,
    grad_text_ref,
    temp_grad_ref,
):
    scale = exp_of(temp_ref[0, 0])
    for source, total, result in (
        (image_ref, sum_image_ref, grad_image_ref),
        (text_ref, sum_text_ref, grad_text_ref),
    ):
        rows = source[...]
        inverse = lax.rsqrt(jnp.sum(rows * rows, axis=1, keepdims=True) + 1e-06)
        grad = total[...].astype(F32) * scale
        unit = rows * inverse
        result[...] = inverse * (grad - unit * jnp.sum(unit * grad, axis=1, keepdims=True))
    totals = totals_ref[...]
    loss_ref[0, 0] = jnp.sum(totals[0:1, :]) * (LN2 / (2.0 * PAIRS))
    temp_grad_ref[0, 0] = jnp.sum(totals[1:2, :]) * (LN2 / PAIRS)


def on_device(image_feat, text_feat, logit_temp):
    logit_temp = logit_temp.reshape(1, 1)
    smem = pl.BlockSpec(memory_space=pltpu.SMEM)
    anywhere = pl.BlockSpec(memory_space=pl.ANY)
    one = jax.ShapeDtypeStruct((1, 1), F32)
    shape = jax.ShapeDtypeStruct((BLOCK, WIDTH), F32)
    low_shape = jax.ShapeDtypeStruct((BLOCK, WIDTH), BF16)
    totals, sum_image, sum_text = pl.pallas_call(
        kernel,
        out_shape=(jax.ShapeDtypeStruct((8, 128), F32), low_shape, low_shape),
        in_specs=[smem, anywhere, anywhere],
        out_specs=(pl.BlockSpec(memory_space=pltpu.VMEM), anywhere, anywhere),
        scratch_shapes=[
            pltpu.VMEM((BLOCK, WIDTH), F32),
            pltpu.VMEM((BLOCK, WIDTH), F32),
            pltpu.VMEM((1024, WIDTH), BF16),
            pltpu.VMEM((2048, WIDTH), BF16),
            pltpu.VMEM((1024, 2048), F32),
            pltpu.VMEM((1024, 2048), BF16),
            pltpu.VMEM((1024, 128), F32),
            pltpu.VMEM((1024, 128), F32),
            pltpu.VMEM((8, 2048), F32),
            pltpu.VMEM((8, 2048), F32),
            pltpu.VMEM((1024, 128), F32),
            pltpu.VMEM((1, 2048), F32),
            pltpu.VMEM((8, BLOCK, BLOCK), F32),
            pltpu.VMEM((8, 128), F32),
            pltpu.VMEM((8, 16, 128), F32),
            pltpu.VMEM((16, 32, 128), F32),
            pltpu.VMEM((8, 8, 128), F32),
            pltpu.VMEM((16, 8, 128), F32),
            pltpu.VMEM((1024, WIDTH), F32),
            pltpu.VMEM((1024, WIDTH), F32),
            pltpu.VMEM((1024, WIDTH), BF16),
            pltpu.VMEM((1024, WIDTH), BF16),
            pltpu.VMEM((1024, WIDTH), BF16),
            pltpu.VMEM((7 * BLOCK, WIDTH), BF16),
            pltpu.VMEM((7 * BLOCK, WIDTH), BF16),
            pltpu.VMEM((1024, WIDTH), BF16),
            pltpu.SemaphoreType.DMA((168,)),
            pltpu.SemaphoreType.DMA((168,)),
            pltpu.SemaphoreType.DMA((4,)),
        ],
        compiler_params=pltpu.CompilerParams(
            collective_id=0, has_side_effects=True, vmem_limit_bytes=60 * 2**20
        ),
        cost_estimate=pl.CostEstimate(flops=16106127360, bytes_accessed=2621440, transcendentals=8388608),
    )(logit_temp, image_feat, text_feat)
    step_rows = 64
    rows = pl.BlockSpec((step_rows, WIDTH), lambda i: (i, 0))
    mean_loss, grad_image, grad_text, temp_grad = pl.pallas_call(
        finalize,
        grid=(BLOCK // step_rows,),
        out_shape=(one, shape, shape, one),
        in_specs=[smem, pl.BlockSpec((8, 128), lambda i: (0, 0)), rows, rows, rows, rows],
        out_specs=(smem, rows, rows, smem),
    )(logit_temp, totals, image_feat, text_feat, sum_image, sum_text)
    return (mean_loss[0, 0], grad_image, grad_text, temp_grad[0, 0])


def solution(mesh):
    in_specs = (P(("img", "txt"), None), P(("txt", "img"), None), P())
    out_specs = (P(), P(("img", "txt"), None), P(("txt", "img"), None), P())
    return jax.shard_map(
        on_device, mesh=mesh, in_specs=in_specs, out_specs=out_specs, check_vma=False
    )
```
